32 devices in a mesh: groups: 2 (over x), obs: 16 (over z, y, core).
Axes of the slice: x: 2, y: 2, z: 4, core: 2. Of those that a mesh axis runs over, the one named last changes fastest.
Arguments:
- footprints: float32 [512, 4, 128, 256], P(('groups', 'obs')), parts along dimension 0, may hold values from -0.1875 to 0.1875
- tile_index: int32 [512, 4], P(('groups', 'obs')), parts along dimension 0, may hold values from 0 to 511, as said below
- observed: float32 [512, 128], P(('groups', 'obs')), parts along dimension 0, may hold values from -6 to 6
- week_ids: int32 [512, 128], P(('groups', 'obs')), parts along dimension 0, may hold values from 0 to 7
- week_weight: float32 [16], P('groups'), parts along dimension 0, may hold values from 0.25 to 4
- counts: int32 [32], P(('groups', 'obs')), parts along dimension 0, may hold values from 1 to 2048, 16384 in all
- flux_start: float32 [1024, 256], P(('groups', 'obs')), parts along dimension 0, may hold values from -6 to 6
- flux_prior: float32 [1024, 256], P(('groups', 'obs')), parts along dimension 0, may hold values from -6 to 6
- prior_precision: float32 [1024, 256], P(('groups', 'obs')), parts along dimension 0, may hold values from 0.3 to 3
Outputs:
- flux: float32 [1024, 256], P(('groups', 'obs')), parts along dimension 0
- departure: float32 [512, 128], P(('groups', 'obs')), parts along dimension 0
The draws below stay inside these ranges and needn't reach their ends.
There are 2 independent parts, one for each index of `groups`. The reference program is written for one: setup_inputs(seed, part) draws one part's arguments, and reference() takes and returns one part's arrays. A program takes and returns all parts, laid end to end along the dimension named above; each array names one. Nothing has to cross between parts.
Inputs may be any that keep to these rules, and one draw needn't show every extreme that they name: `tile_index`: for every device, the 64 tiles of its sounding blocks name flux blocks of any one device's share (blocks j * 32 to (j + 1) * 32 - 1) at most 8 times, and some share exactly 8 times. In each part of groups the counts sum to 16384, and the largest is 2048.
All inputs are finite; a program needn't handle non-finite values.
Results may differ from the reference program's by a relative error of at most 0.0001.
Values sent between devices are 32-bit elements; how exact they have to be, the bound alone decides.
No kernel may reach another device: no remote copies, remote signals or barrier semaphores. Data moves between devices by JAX's collectives and lax.ppermute only.
A program may use at most 64 MiB of HBM per device.

```python
import math
import jax
import jax.numpy as jnp
import numpy as np
from jax import lax

TR = 128
TC = 256
KT = 4
WEEKS = 8
ITERS = 2
SB_DEV = 16
FB_DEV = 32
CAP = 8
NSB = 256
NFB = 512
N_OBS = 16


def draw_tile_index(key, part):
    key = jax.random.fold_in(key, 11)
    tile_count = SB_DEV * KT

    def per_device(device):
        device_key = jax.random.fold_in(key, device)
        key_pick, key_order, key_local = jax.random.split(device_key, 3)
        picks = jax.random.permutation(key_pick, (N_OBS - 1) * CAP)[:tile_count - CAP]
        others = (device + 2 + picks // CAP) % N_OBS
        owners = jnp.concatenate([jnp.full((CAP,), (device + 1) % N_OBS, jnp.int32), others.astype(jnp.int32)])
        owners = jax.random.permutation(key_order, owners)
        local_ids = jax.random.randint(key_local, (tile_count,), 0, FB_DEV)
        return (owners * FB_DEV + local_ids).astype(jnp.int32).reshape(SB_DEV, KT)
    drawn = jax.vmap(per_device)(jnp.arange(N_OBS, dtype=jnp.int32))
    return drawn.reshape(SB_DEV * N_OBS, KT).astype(jnp.int32)


def touch_ends(result, rng, least, top_value):
    place = [jax.random.randint(jax.random.fold_in(rng, axis), (), 0, length) for axis, length in enumerate(result.shape)]
    longest = result.shape.index(max(result.shape))
    beside = place[:longest] + [(place[longest] + 1) % result.shape[longest]] + place[longest + 1:]
    return result.at[tuple(place)].set(least).at[tuple(beside)].set(top_value)


def levels(rng, extent, cuts, smallest, largest):
    level, own = 1.0, jax.random.fold_in(rng, 6)
    for dim, blocks in cuts:
        heights = jnp.exp(jax.random.uniform(jax.random.fold_in(own, dim), (blocks,), jnp.float32, smallest / len(cuts), largest / len(cuts)))
        level = level * jnp.repeat(heights, extent[dim] // blocks).reshape([-1 if axis == dim else 1 for axis in range(len(extent))])
    return level


def profile(amount, total, limit, skew):
    weights = [(1 << 20) // math.isqrt(grade ** skew) + 1 for grade in range(2, amount + 1)]
    spare, holding = total - limit - (amount - 1), [1] * (amount - 1)
    while spare > 0:
        movable = [i for i in range(amount - 1) if holding[i] < limit]
        mass, left = sum([weights[i] for i in movable]), spare
        for i in movable:
            more = min(limit - holding[i], max(1, left * weights[i] // mass), spare)
            holding[i] = holding[i] + more
            spare = spare - more
    return np.array([limit] + holding)


def uneven_parts(own_key, amount, total, reach, slope):
    if amount == 2:
        one = jax.random.randint(own_key, (), max(1, total - reach), min(reach, total - 1) + 1)
        return jnp.stack([one, total - one])
    sizes = jnp.asarray(profile(amount, total, reach, slope), jnp.int32)
    pairs = (amount - 1) // 2
    source_of, sink = sizes[1:1 + 2 * pairs:2], sizes[2:2 + 2 * pairs:2]
    slack = jnp.minimum(source_of - 1, reach - sink)
    passed = jax.random.randint(jax.random.fold_in(own_key, 1), (pairs,), 0, 1 << 20) % (slack + 1)
    sizes = sizes.at[1:1 + 2 * pairs:2].set(source_of - passed).at[2:2 + 2 * pairs:2].set(sink + passed)
    return sizes[jax.random.permutation(jax.random.fold_in(own_key, 2), amount)]


def bell_draw(stream_key, shape, deviation, limit, pieces=(), held_as=jnp.bfloat16):
    values = jax.random.normal(stream_key, shape, jnp.float32) * deviation
    if len(pieces) > 0:
        values = levels(stream_key, shape, pieces, -0.22, 0.18) * values
    return jnp.clip(values, min=-limit, max=limit).astype(held_as)


def setup_inputs(seed: int = 0, part: int = 0) -> dict:
    seeds = jax.random.split(jax.random.key(seed), 10)
    part_keys = jax.random.split(jax.random.fold_in(seeds[9], part), 10)
    footprints = bell_draw(part_keys[0], (NSB, KT, TR, TC), (KT * TC) ** -0.5, 0.1875, ((0, 16),), jnp.float32)
    tile_index = draw_tile_index(jax.random.fold_in(jax.random.fold_in(seeds[9], part), 71), part)
    observed = bell_draw(part_keys[2], (NSB, TR), 1.0, 6.0, ((0, 16),), jnp.float32)
    week_ids = touch_ends(jax.random.randint(part_keys[3], (NSB, TR), 0, WEEKS), jax.random.fold_in(part_keys[3], 1), 0, WEEKS - 1).astype(jnp.int32)
    week_weight = jnp.clip(jnp.exp(jax.random.uniform(part_keys[4], (WEEKS,), jnp.float32, math.log(0.25), math.log(4.0))), 0.25, 4.0)
    counts = uneven_parts(part_keys[5], N_OBS, N_OBS * SB_DEV * TR // 2, SB_DEV * TR, 2).astype(jnp.int32)
    flux_start = bell_draw(part_keys[6], (NFB, TC), 1.0, 6.0, ((0, 16),), jnp.float32)
    flux_prior = bell_draw(part_keys[7], (NFB, TC), 1.0, 6.0, ((0, 16),), jnp.float32)
    prior_precision = jnp.clip(jnp.exp(math.log(3.0) - 2.3025851 * jax.random.uniform(part_keys[8], (NFB, TC), jnp.float32) ** levels(part_keys[8], (NFB, TC), ((0, 16),), -0.2, 0.2)), 0.3, 3.0)
    return {"footprints": footprints, "tile_index": tile_index, "observed": observed, "week_ids": week_ids, "week_weight": week_weight, "counts": counts, "flux_start": flux_start, "flux_prior": flux_prior, "prior_precision": prior_precision}


def forward(footprints, tile_index, values):
    blocks = values[tile_index]
    return jnp.einsum("bkrc,bkc->br", footprints, blocks, precision=lax.Precision.HIGHEST)


def transpose(footprints, tile_index, residual):
    adjoint_terms = jnp.einsum("bkrc,br->bkc", footprints, residual, precision=lax.Precision.HIGHEST)
    total = jnp.zeros((NFB, TC), jnp.float32)
    return total.at[tile_index.reshape(-1)].add(adjoint_terms.reshape(-1, TC))


def reference(footprints, tile_index, observed, week_ids, week_weight, counts, flux_start, flux_prior, prior_precision):
    block_rows = jnp.arange(NSB, dtype=jnp.int32)
    device_of = block_rows // SB_DEV
    positions = (block_rows % SB_DEV)[:, None] * TR + jnp.arange(TR, dtype=jnp.int32)[None, :]
    live_rows = (positions < counts[device_of][:, None]).astype(jnp.float32)
    week_table = (week_ids[:, :, None] == jnp.arange(WEEKS, dtype=jnp.int32)[None, None, :]).astype(jnp.float32)
    weights = live_rows * jnp.sum(week_table * week_weight, axis=2)
    flux = flux_start
    departure = forward(footprints, tile_index, flux) - observed
    for sweep in range(ITERS):
        gradient = transpose(footprints, tile_index, weights * departure) + prior_precision * (flux - flux_prior)
        image = forward(footprints, tile_index, gradient)
        grad_square = jnp.sum(gradient * gradient)
        grad_prior = jnp.sum(prior_precision * gradient * gradient)
        fit_curve = jnp.sum(weights * image * image)
        step_size = grad_square / (fit_curve + grad_prior)
        flux = flux - step_size * gradient
        departure = departure - step_size * image
    return flux, departure
```

```python
import functools

import jax
import jax.numpy as jnp
from jax import lax
from jax.experimental import pallas as pl
from jax.experimental.pallas import tpu as pltpu
from jax.sharding import PartitionSpec as P

VMEM = pl.BlockSpec(memory_space=pltpu.VMEM)
SMEM = pl.BlockSpec(memory_space=pltpu.SMEM)
ANY = pl.BlockSpec(memory_space=pl.ANY)
LIMIT = 40 * 1024 * 1024


def stage_masks(n):
    stages, low = [], 1
    while low < n:
        if low < 4 or low * 4 > n:
            stages.append([low])
            low *= 2
        else:
            stages.append([low, 2 * low, 3 * low])
            low *= 4
    return stages[::-1]


def piece_order(n):
    order = [0]
    for masks in stage_masks(n):
        order = order + [m ^ o for m in masks for o in order]
    return order


def swap(x, mask):
    n = lax.axis_size("obs")
    return lax.ppermute(x, "obs", [(i, i ^ mask) for i in range(n)])


def spread(x):
    stages = stage_masks(lax.axis_size("obs"))
    for masks in stages[:-1]:
        x = jnp.concatenate([x] + [swap(x, m) for m in masks], axis=0)
    return x, swap(x, stages[-1][0])


def prepare_kernel(week_weight, counts, week_ids, observed, w_out, y_out):
    blocks, rows = week_ids.shape
    ids = week_ids[...]
    table = jnp.zeros(ids.shape, jnp.float32)
    for week in range(week_weight.shape[0]):
        table = jnp.where(ids == week, week_weight[week], table)
    position = lax.broadcasted_iota(jnp.int32, ids.shape, 0) * rows + lax.broadcasted_iota(jnp.int32, ids.shape, 1)
    weights = jnp.where(position < counts[0], table, 0.0)
    fill = jnp.zeros((rows - blocks, rows), jnp.float32)
    w_out[...] = jnp.concatenate([weights, fill], axis=0).T
    y_out[...] = jnp.concatenate([observed[...], fill], axis=0).T


def forward_block(tiles, values, lane, b, minus):
    total = None
    for k, v in enumerate(values):
        part = tiles[b, k] * v
        total = part if total is None else total + part
    half = total.shape[1] // 2
    total = total[:, :half] + total[:, half:]
    if minus is not None:
        total = total - jnp.where(lane == b, minus, 0.0)
    return jnp.sum(total, axis=1, keepdims=True)


def start_tiles(footprints, tiles, sem):
    @pl.loop(0, tiles.shape[0])
    def _(b):
        pltpu.make_async_copy(footprints.at[b], tiles.at[b], sem.at[b]).start()


def first_kernel(rows, low, high, footprints, weights, observed, terms_out, departure_out, tiles, sem):
    start_tiles(footprints, tiles, sem)
    blocks, each, tile_rows, _ = tiles.shape
    lane = lax.broadcasted_iota(jnp.int32, (tile_rows, tile_rows), 1)
    departure_out[...] = jnp.zeros_like(departure_out)
    half = low.shape[0]

    @pl.loop(0, blocks)
    def _(b):
        pltpu.make_async_copy(footprints.at[b], tiles.at[b], sem.at[b]).wait()
        values = []
        for k in range(each):
            row = rows[b * each + k]
            a = low[pl.ds(jnp.minimum(row, half - 1), 1), :]
            z = high[pl.ds(jnp.maximum(row - half, 0), 1), :]
            values.append(jnp.where(row < half, a, z))
        depart = forward_block(tiles, values, lane, b, observed[...])
        departure_out[...] = jnp.where(lane == b, depart, departure_out[...])
        w = jnp.sum(jnp.where(lane == b, weights[...], 0.0), axis=1, keepdims=True)
        scaled = w * depart
        for k in range(each):
            terms_out[pl.ds(b * each + k, 1), :] = jnp.sum(tiles[b, k] * scaled, axis=0, keepdims=True)


def gather_terms(order, me, want, static, low, high, piece, hot):
    lane = lax.broadcasted_iota(jnp.int32, (1, 128), 1)
    wanted = want[...]
    ids_row = static.shape[1] - 8
    for q in range(len(order) // 2):
        first = static[me ^ order[2 * q], pl.ds(ids_row, 1), :128]
        second = static[me ^ order[2 * q + 1], pl.ds(ids_row, 1), :128]
        ids = jnp.where(lane < 64, first, second)
        hot[:, q * 128:(q + 1) * 128] = jnp.where(wanted == ids, 1.0, 0.0)
    each = len(order) // 2
    total = jnp.zeros((wanted.shape[0], low.shape[-1]), jnp.float32)
    for i, part in enumerate((low, high)):
        if part.shape[0] == each * piece:
            block = part[...]
        else:
            pitch = part.shape[0] // each
            block = jnp.concatenate([part[j * pitch:j * pitch + piece, :] for j in range(each)], axis=0)
        total = total + jnp.dot(
            hot[:, i * each * piece:(i + 1) * each * piece], block,
            precision=lax.Precision.HIGHEST, preferred_element_type=jnp.float32)
    return total


def second_kernel(order, tile_ids, me, want, static, low, high, footprints, weights, c_own, precision,
                  terms_out, gradient_out, image_out, tiles, sem, hot):
    start_tiles(footprints, tiles, sem)
    blocks, each, tile_rows, _ = tiles.shape
    count = blocks * each
    own = c_own.shape[0]
    lane = lax.broadcasted_iota(jnp.int32, (tile_rows, tile_rows), 1)
    image_out[...] = jnp.zeros_like(image_out)
    gradient_out[...] = gather_terms(order, me[0], want, static, low, high, count, hot)

    @pl.loop(0, count)
    def _(t):
        row = tile_ids[t]
        more = static[row // own, pl.ds(row % own, 1), :]
        gradient_out[pl.ds(t, 1), :] = gradient_out[pl.ds(t, 1), :] + more

    mine = gradient_out[count:, :] + c_own[...]
    gradient_out[count:, :] = mine

    @pl.loop(0, blocks)
    def _(b):
        pltpu.make_async_copy(footprints.at[b], tiles.at[b], sem.at[b]).wait()
        values = [gradient_out[pl.ds(b * each + k, 1), :] for k in range(each)]
        image = forward_block(tiles, values, lane, b, None)
        image_out[...] = jnp.where(lane == b, image, image_out[...])
        w = jnp.sum(jnp.where(lane == b, weights[...], 0.0), axis=1, keepdims=True)
        scaled = w * image
        for k in range(each):
            terms_out[pl.ds(b * each + k, 1), :] = jnp.sum(tiles[b, k] * scaled, axis=0, keepdims=True)

    image = image_out[...]
    terms_out[count:, :] = sums_row(mine, precision[...], weights[...], image, (8, terms_out.shape[1]))


def sums_row(gradient, precision, weights, image, shape):
    square = jnp.sum(gradient * gradient)
    below = jnp.sum(precision * gradient * gradient) + jnp.sum(weights * image * image)
    lane = lax.broadcasted_iota(jnp.int32, shape, 1)
    return jnp.where(lane == 0, square, jnp.where(lane == 1, below, 0.0))


def third_kernel(order, tile_ids, me, want, static, low, high, footprints, weights, precision, gradient,
                 departure, image, flux,
                 sums_out, flux_out, gradient_out, departure_out, image_out, tiles, sem, hot, second):
    start_tiles(footprints, tiles, sem)
    blocks, each, tile_rows, _ = tiles.shape
    count = blocks * each
    own = flux.shape[0]
    n = len(order)
    lane = lax.broadcasted_iota(jnp.int32, (tile_rows, tile_rows), 1)
    second[...] = gather_terms(order, me[0], want, static, low, high, count, hot)
    pitch = low.shape[0] // (n // 2)
    sums = jnp.zeros((1, 128), jnp.float32)
    for part in (low, high):
        for j in range(n // 2):
            sums = sums + part[j * pitch + count:j * pitch + count + 1, :128]
    step = sums[:, 0:1] / sums[:, 1:2]

    @pl.loop(0, count)
    def _(t):
        row = tile_ids[t]
        scale = static[row // own, pl.ds(own + row % own, 1), :]
        old = gradient[pl.ds(t, 1), :]
        second[pl.ds(t, 1), :] = old - step * (second[pl.ds(t, 1), :] + scale * old)

    old = gradient[count:, :]
    mine = old - step * (second[count:, :] + precision[...] * old)
    gradient_out[...] = mine
    flux_out[...] = flux[...] - step * old
    columns = jnp.zeros((tile_rows, tile_rows), jnp.float32)

    def block(b, columns):
        pltpu.make_async_copy(footprints.at[b], tiles.at[b], sem.at[b]).wait()
        values = [second[pl.ds(b * each + k, 1), :] for k in range(each)]
        return jnp.where(lane == b, forward_block(tiles, values, lane, b, None), columns)

    columns = lax.fori_loop(0, blocks, block, columns)
    row = sums_row(mine, precision[...], weights[...], columns, (1, 128))
    sums_out[...] = jnp.broadcast_to(row[None], sums_out.shape)
    departure_out[...] = (departure[...] - step * image[...]).T[:blocks]
    image_out[...] = columns.T[:blocks]


def last_kernel(sums, flux, gradient, departure, image, flux_out, departure_out):
    total = jnp.sum(sums[...], axis=0)
    step = total[:, 0:1] / total[:, 1:2]
    flux_out[...] = flux[...] - step * gradient[...]
    departure_out[...] = departure[...] - step * image[...]


def call(kernel, ins, outs, scratch=(), flops=0, moved=0):
    return pl.pallas_call(
        kernel,
        out_shape=[jax.ShapeDtypeStruct(s, jnp.float32) for s in outs],
        in_specs=ins,
        out_specs=[VMEM] * len(outs),
        scratch_shapes=list(scratch),
        compiler_params=pltpu.CompilerParams(vmem_limit_bytes=LIMIT),
        cost_estimate=pl.CostEstimate(flops=flops, bytes_accessed=moved, transcendentals=0),
    )


def body(footprints, tile_index, observed, week_ids, week_weight, counts, flux_start, flux_prior, prior_precision):
    n = lax.axis_size("obs")
    me = lax.axis_index("obs").astype(jnp.int32)
    blocks, each, tile_rows, cols = footprints.shape
    own = flux_start.shape[0]
    count = blocks * each
    order = piece_order(n)

    low, high = spread(flux_start)

    flat = tile_index.reshape(-1)
    c_own = prior_precision * (flux_start - flux_prior)
    ids = jnp.tile(flat.astype(jnp.float32), cols // count)
    mine = jnp.concatenate([c_own, prior_precision, jnp.broadcast_to(ids[None], (8, cols))], axis=0)
    static = lax.all_gather(mine, "obs", axis=0)
    want = jnp.concatenate([flat, me * own + jnp.arange(own, dtype=jnp.int32)]).astype(jnp.float32)[:, None]
    distance = jnp.bitwise_xor(flat // own, me)
    place = jnp.zeros_like(flat)
    for at, o in enumerate(order):
        place = jnp.where(distance == o, at, place)
    rows = place * own + flat % own
    me_s = me[None]

    weights, observed_t = call(
        prepare_kernel, [SMEM, SMEM, VMEM, VMEM], [(tile_rows, tile_rows)] * 2, flops=10000, moved=200000,
    )(week_weight, counts, week_ids, observed)

    tiles = [pltpu.VMEM(footprints.shape, jnp.float32), pltpu.SemaphoreType.DMA((blocks,))]
    hot = pltpu.VMEM((count + own, n * count), jnp.float32)
    work = dict(flops=4 * footprints.size, moved=4 * footprints.size)

    terms, departure = call(
        first_kernel, [SMEM, VMEM, VMEM, ANY, VMEM, VMEM],
        [(count, cols), (tile_rows, tile_rows)], tiles, **work,
    )(rows, low, high, footprints, weights, observed_t)

    low, high = spread(terms)
    terms, gradient, image = call(
        functools.partial(second_kernel, order),
        [SMEM, SMEM, VMEM, VMEM, VMEM, VMEM, ANY, VMEM, VMEM, VMEM],
        [(count + 8, cols), (count + own, cols), (tile_rows, tile_rows)], tiles + [hot], **work,
    )(flat, me_s, want, static, low, high, footprints, weights, c_own, prior_precision)

    low, high = spread(terms)
    sums, flux, gradient, departure, image = call(
        functools.partial(third_kernel, order),
        [SMEM, SMEM, VMEM, VMEM, VMEM, VMEM, ANY] + [VMEM] * 6,
        [(n, 1, 128), (own, cols), (own, cols), (blocks, tile_rows), (blocks, tile_rows)],
        tiles + [hot, pltpu.VMEM((count + own, cols), jnp.float32)], **work,
    )(flat, me_s, want, static, low, high, footprints, weights, prior_precision, gradient, departure, image,
      flux_start)

    sums = lax.all_to_all(sums, "obs", 0, 0)
    flux, departure = call(
        last_kernel, [VMEM] * 5, [(own, cols), (blocks, tile_rows)], flops=20000, moved=200000,
    )(sums, flux, gradient, departure, image)
    return flux, departure


def solution(mesh):
    rows = P(("groups", "obs"), None)
    return jax.shard_map(
        body,
        mesh=mesh,
        in_specs=(
            P(("groups", "obs"), None, None, None), rows, rows, rows,
            P("groups"), P(("groups", "obs")), rows, rows, rows,
        ),
        out_specs=(rows, rows),
        check_vma=False,
    )
```

```python
import functools

import jax
import jax.numpy as jnp
from jax import lax
from jax.experimental import pallas as pl
from jax.experimental.pallas import tpu as pltpu
from jax.sharding import PartitionSpec as P

VMEM = pl.BlockSpec(memory_space=pltpu.VMEM)
SMEM = pl.BlockSpec(memory_space=pltpu.SMEM)
ANY = pl.BlockSpec(memory_space=pl.ANY)
HBM = pl.BlockSpec(memory_space=pltpu.HBM)
LIMIT = 24 * 1024 * 1024
F32 = jnp.float32


def stage_masks(n):
    stages, low = [], 1
    while low < n:
        if low < 4 or low * 4 > n:
            stages.append([low])
            low *= 2
        else:
            stages.append([low, 2 * low, 3 * low])
            low *= 4
    return stages[::-1]


def swap(x, mask):
    n = lax.axis_size("obs")
    return lax.ppermute(x, "obs", [(i, i ^ mask) for i in range(n)])


def shift(masks, mask):
    return [m ^ mask for m in masks]


def call(kernel, ins, outs, scratch=(), flops=0, moved=0, pinned=False):
    return pl.pallas_call(
        kernel,
        out_shape=[pltpu.VMEM(s, F32) if pinned and len(s) == 4 else jax.ShapeDtypeStruct(s, F32) for s in outs],
        in_specs=ins,
        out_specs=[VMEM] * len(outs),
        scratch_shapes=list(scratch),
        compiler_params=pltpu.CompilerParams(vmem_limit_bytes=LIMIT),
        cost_estimate=pl.CostEstimate(flops=flops, bytes_accessed=moved, transcendentals=0),
    )


def pile_kernel(pitch, at, rows, *refs):
    *arrays, _, pile_out = refs
    i = 0
    for array in arrays:
        for start in range(0, array.shape[0], pitch):
            pile_out[i:i + rows, :] = array[start + at:start + at + rows, :]
            i += rows


def pile(arrays, pitch, at, rows, after):
    total = sum(a.shape[0] for a in arrays) // pitch * rows
    cols = arrays[0].shape[1]
    return call(
        functools.partial(pile_kernel, pitch, at, rows), [VMEM] * len(arrays) + [ANY], [(total, cols)],
        moved=8 * total * cols,
    )(*arrays, after)[0]


def far_stages(x, pitch, after):
    masks = [0]
    *lead, last = stage_masks(lax.axis_size("obs"))[:-2]
    for stage in lead:
        x = pile([x] + [swap(x, m) for m in stage], pitch, 0, pitch, after)
        masks = masks + [k for m in stage for k in shift(masks, m)]
    if len(last) == 1:
        return [([x], masks), ([swap(x, last[0])], shift(masks, last[0]))]
    near, *rest = last
    far = [swap(x, m) for m in rest]
    return [
        ([x, swap(x, near)], masks + shift(masks, near)),
        (far, [k for m in rest for k in shift(masks, m)]),
    ]


def near_stages(halves):
    last = stage_masks(lax.axis_size("obs"))[-2:]
    parts = list(halves)
    for (m,) in last:
        parts = parts + [(swap(x, m), shift(masks, m)) for x, masks in parts]
    return [x for x, _ in parts], [masks for _, masks in parts]


def spread(x):
    rows = x.shape[0]
    return near_stages([(pile(a, rows, 0, rows, x), m) for a, m in far_stages(x, rows, x)])


def bundle_kernel(tile_ids, me, flux, prior, precision, bundle_out, want_out, prior_in, sem):
    each, blocks = tile_ids.shape
    count = blocks * each
    own, cols = flux.shape
    copies = [
        pltpu.make_async_copy(flux, bundle_out.at[pl.ds(0, own)], sem.at[0]),
        pltpu.make_async_copy(precision, bundle_out.at[pl.ds(2 * own, own)], sem.at[1]),
        pltpu.make_async_copy(prior, prior_in, sem.at[2]),
    ]
    for c in copies:
        c.start()
    lane = lax.broadcasted_iota(jnp.int32, (8, cols), 1) % count
    tall = lax.broadcasted_iota(jnp.int32, want_out.shape, 0)
    across = jnp.zeros((8, cols), jnp.int32)
    down = me[0] * own + tall - count
    for t in range(count):
        tile = tile_ids[t % each, t // each]
        across = jnp.where(lane == t, tile, across)
        down = jnp.where(tall == t, tile, down)
    bundle_out[3 * own:, :] = across.astype(F32)
    want_out[...] = down.astype(F32)
    for c in copies:
        c.wait()
    bundle_out[own:2 * own, :] = bundle_out[2 * own:3 * own, :] * (bundle_out[:own, :] - prior_in[...])


def prepare_kernel(tile_ids, me, week_weight, counts, week_ids, observed, footprints, w_out, y_out, tiles_out,
                   ids_in, y_in, sem):
    del tile_ids, me
    small = [
        pltpu.make_async_copy(week_ids, ids_in, sem.at[0]),
        pltpu.make_async_copy(observed, y_in, sem.at[1]),
    ]
    copy = pltpu.make_async_copy(footprints, tiles_out, sem.at[2])
    for c in small:
        c.start()
    copy.start()
    for c in small:
        c.wait()
    blocks, rows = week_ids.shape
    ids = ids_in[...]
    table = jnp.zeros(ids.shape, F32)
    for week in range(week_weight.shape[0]):
        table = jnp.where(ids == week, week_weight[week], table)
    position = lax.broadcasted_iota(jnp.int32, ids.shape, 0) * rows + lax.broadcasted_iota(jnp.int32, ids.shape, 1)
    weights = jnp.where(position < counts[0], table, 0.0)
    fill = jnp.zeros((rows - blocks, rows), F32)
    w_out[...] = jnp.concatenate([weights, fill], axis=0).T
    y_out[...] = jnp.concatenate([y_in[...], fill], axis=0).T
    copy.wait()


def by_owner(me, masks, refs, pitch, at, rows, into):
    for ref, ms in zip(refs, masks, strict=True):
        for j, m in enumerate(ms):
            place = pl.ds(pl.multiple_of((me ^ m) * rows, 8), rows)
            into[place, :] = ref[j * pitch + at:j * pitch + at + rows, :]


def forward_block(tiles, values, lane, b, minus):
    total = None
    for k, v in enumerate(values):
        part = tiles[b, k] * v
        total = part if total is None else total + part
    half = total.shape[1] // 2
    total = total[:, :half] + total[:, half:]
    if minus is not None:
        total = total - jnp.where(lane == b, minus, 0.0)
    return jnp.sum(total, axis=1, keepdims=True)


def transpose_block(tiles, weights, column, lane, b, terms_out):
    w = jnp.sum(jnp.where(lane == b, weights[...], 0.0), axis=1, keepdims=True)
    scaled = w * column
    each = tiles.shape[1]
    for k in range(each):
        terms_out[pl.ds(b * each + k, 1), :] = jnp.sum(tiles[b, k] * scaled, axis=0, keepdims=True)


def first_kernel(masks, tile_ids, me, tiles, weights, observed, *refs):
    *parts, terms_out, departure_out, flux = refs
    blocks, each, tile_rows, _ = tiles.shape
    own = parts[0].shape[0] // len(masks[0])
    by_owner(me[0], masks, parts, own, 0, own, flux)
    lane = lax.broadcasted_iota(jnp.int32, (tile_rows, tile_rows), 1)
    departure_out[...] = jnp.zeros_like(departure_out)

    @pl.loop(0, blocks, unroll=4)
    def _(b):
        values = [flux[pl.ds(tile_ids[k, b], 1), :] for k in range(each)]
        depart = forward_block(tiles, values, lane, b, observed[...])
        departure_out[...] = jnp.where(lane == b, depart, departure_out[...])
        transpose_block(tiles, weights, depart, lane, b, terms_out)


def sum_terms(masks, parts, piece, name_masks, names, want, hot):
    lane = lax.broadcasted_iota(jnp.int32, (1, 128), 1)
    wanted = want[...]
    ids = {}
    for ref, ms in zip(names, name_masks, strict=True):
        pitch = ref.shape[0] // len(ms)
        for j, m in enumerate(ms):
            ids[m] = ref[(j + 1) * pitch - 8:(j + 1) * pitch - 7, :128]
    order = [m for ms in masks for m in ms]
    for j in range(0, len(order), 2):
        pair = jnp.where(lane < piece, ids[order[j]], ids[order[j + 1]])
        hot[:, j * piece:(j + 2) * piece] = jnp.where(wanted == pair, 1.0, 0.0)
    pitch = parts[0].shape[0] // len(masks[0])
    block = jnp.concatenate(
        [ref[j * pitch:j * pitch + piece, :] for ref, ms in zip(parts, masks, strict=True) for j in range(len(ms))], axis=0)
    return jnp.dot(hot[...], block, precision=lax.Precision.HIGHEST, preferred_element_type=F32)


def sums_row(gradient, precision, weights, image, shape):
    square = jnp.sum(gradient * gradient)
    below = jnp.sum(precision * gradient * gradient) + jnp.sum(weights * image * image)
    lane = lax.broadcasted_iota(jnp.int32, shape, 1)
    return jnp.where(lane == 0, square, jnp.where(lane == 1, below, 0.0))


def second_kernel(masks, name_masks, tile_ids, me, tiles, weights, want, bundle, *refs):
    parts, names = refs[:len(masks)], refs[len(masks):len(masks) + len(name_masks)]
    terms_out, gradient_out, image_out, hot, more = refs[len(masks) + len(name_masks):]
    blocks, each, tile_rows, _ = tiles.shape
    count = blocks * each
    own = want.shape[0] - count
    by_owner(me[0], name_masks, names, 2 * own + 8, 0, own, more)
    lane = lax.broadcasted_iota(jnp.int32, (tile_rows, tile_rows), 1)
    image_out[...] = jnp.zeros_like(image_out)
    gradient_out[...] = sum_terms(masks, parts, count, name_masks, names, want, hot)
    mine = gradient_out[count:, :] + bundle[own:2 * own, :]
    gradient_out[count:, :] = mine

    @pl.loop(0, blocks, unroll=4)
    def _(b):
        values = []
        for k in range(each):
            t = pl.ds(b * each + k, 1)
            value = gradient_out[t, :] + more[pl.ds(tile_ids[k, b], 1), :]
            gradient_out[t, :] = value
            values.append(value)
        image = forward_block(tiles, values, lane, b, None)
        image_out[...] = jnp.where(lane == b, image, image_out[...])
        transpose_block(tiles, weights, image, lane, b, terms_out)

    terms_out[count:, :] = sums_row(
        mine, bundle[2 * own:3 * own, :], weights[...], image_out[...], (8, terms_out.shape[1]))


def third_kernel(masks, name_masks, tile_ids, me, tiles, weights, want, bundle, gradient, departure, image, *refs):
    parts, names = refs[:len(masks)], refs[len(masks):len(masks) + len(name_masks)]
    (sums_out, flux_out, gradient_out, departure_out, image_out, hot, scale, second) = refs[len(masks) + len(name_masks):]
    blocks, each, tile_rows, _ = tiles.shape
    count = blocks * each
    own = want.shape[0] - count
    by_owner(me[0], name_masks, names, 2 * own + 8, own, own, scale)
    lane = lax.broadcasted_iota(jnp.int32, (tile_rows, tile_rows), 1)
    pitch = parts[0].shape[0] // len(masks[0])
    sums = jnp.zeros((1, 128), F32)
    for ref, ms in zip(parts, masks, strict=True):
        for j in range(len(ms)):
            sums = sums + ref[j * pitch + count:j * pitch + count + 1, :128]
    step = sums[:, 0:1] / sums[:, 1:2]
    second[...] = sum_terms(masks, parts, count, name_masks, names, want, hot)
    old = gradient[count:, :]
    precision = bundle[2 * own:3 * own, :]
    mine = old - step * (second[count:, :] + precision * old)
    gradient_out[...] = mine
    flux_out[...] = bundle[:own, :] - step * old
    second[:count, :] = gradient[:count, :] - step * second[:count, :]

    def block(b, columns):
        values = []
        for k in range(each):
            t = pl.ds(b * each + k, 1)
            values.append(second[t, :] - step * scale[pl.ds(tile_ids[k, b], 1), :] * gradient[t, :])
        return jnp.where(lane == b, forward_block(tiles, values, lane, b, None), columns)

    columns = lax.fori_loop(0, blocks, block, jnp.zeros((tile_rows, tile_rows), F32), unroll=4)
    row = sums_row(mine, precision, weights[...], columns, (1, 128))
    sums_out[...] = jnp.broadcast_to(row[None], sums_out.shape)
    departure_out[...] = (departure[...] - step * image[...]).T[:blocks]
    image_out[...] = columns.T[:blocks]


def last_kernel(sums, flux, gradient, departure, image, flux_out, departure_out):
    total = jnp.sum(sums[...], axis=0)
    step = total[:, 0:1] / total[:, 1:2]
    flux_out[...] = flux[...] - step * gradient[...]
    departure_out[...] = departure[...] - step * image[...]


def body(footprints, tile_index, observed, week_ids, week_weight, counts, flux_start, flux_prior, prior_precision):
    n = lax.axis_size("obs")
    blocks, each, tile_rows, cols = footprints.shape
    own = flux_start.shape[0]
    count = blocks * each
    square = (tile_rows, tile_rows)
    place = (tile_index.T, lax.axis_index("obs").astype(jnp.int32)[None])

    def in_hbm(*arrays):
        return [pltpu.with_memory_space_constraint(x, pltpu.HBM) for x in arrays]

    pitch = 3 * own + 8
    bundle, want = call(
        bundle_kernel, [SMEM] * 2 + [HBM] * 3, [(pitch, cols), (count + own, 128)],
        [pltpu.VMEM((own, cols), F32), pltpu.SemaphoreType.DMA((3,))], flops=10000, moved=12 * own * cols,
    )(*place, *in_hbm(flux_start, flux_prior, prior_precision))
    weights, observed_t, tiles = call(
        prepare_kernel, [SMEM] * 4 + [HBM] * 3, [square, square, footprints.shape],
        [pltpu.VMEM(week_ids.shape, jnp.int32), pltpu.VMEM(observed.shape, F32), pltpu.SemaphoreType.DMA((3,))],
        flops=10000, moved=8 * footprints.size, pinned=True,
    )(*place, week_weight, counts, *in_hbm(week_ids, observed, footprints))
    tiles = pltpu.with_memory_space_constraint(tiles, pltpu.VMEM)

    halves = far_stages(bundle, pitch, bundle)
    parts, masks = near_stages([(pile(a, pitch, 0, own, weights), m) for a, m in halves])

    hot = pltpu.VMEM((count + own, n * count), F32)
    whole = pltpu.VMEM((n * own, cols), F32)
    work = dict(flops=4 * footprints.size, moved=4 * footprints.size)
    terms, departure = call(
        functools.partial(first_kernel, masks), [SMEM] * 2 + [VMEM] * (3 + len(parts)),
        [(count, cols), square], [whole], **work,
    )(*place, tiles, weights, observed_t, *parts)

    rows = 2 * own + 8
    names, name_masks = near_stages(
        [(pile([x for a, _ in halves for x in a], pitch, own, rows, terms), [m for _, ms in halves for m in ms])])
    parts, masks = spread(terms)
    terms, gradient, image = call(
        functools.partial(second_kernel, masks, name_masks), [SMEM] * 2 + [VMEM] * (4 + len(parts) + len(names)),
        [(count + 8, cols), (count + own, cols), square], [hot, whole], **work,
    )(*place, tiles, weights, want, bundle, *parts, *names)

    parts, masks = spread(terms)
    sums, flux, gradient, departure, image = call(
        functools.partial(third_kernel, masks, name_masks), [SMEM] * 2 + [VMEM] * (7 + len(parts) + len(names)),
        [(n, 1, 128), (own, cols), (own, cols), (blocks, tile_rows), (blocks, tile_rows)],
        [hot, whole, pltpu.VMEM((count + own, cols), F32)], **work,
    )(*place, tiles, weights, want, bundle, gradient, departure, image, *parts, *names)

    sums = lax.all_to_all(sums, "obs", 0, 0)
    flux, departure = call(
        last_kernel, [VMEM] * 5, [(own, cols), (blocks, tile_rows)], flops=20000, moved=200000,
    )(sums, flux, gradient, departure, image)
    return flux, departure


def solution(mesh):
    rows = P(("groups", "obs"), None)
    return jax.shard_map(
        body,
        mesh=mesh,
        in_specs=(
            P(("groups", "obs"), None, None, None), rows, rows, rows,
            P("groups"), P(("groups", "obs")), rows, rows, rows,
        ),
        out_specs=(rows, rows),
        check_vma=False,
    )
```

```python
import functools

import jax
import jax.numpy as jnp
from jax import lax
from jax.experimental import pallas as pl
from jax.experimental.pallas import tpu as pltpu
from jax.sharding import PartitionSpec as P

VMEM = pl.BlockSpec(memory_space=pltpu.VMEM)
SMEM = pl.BlockSpec(memory_space=pltpu.SMEM)
ANY = pl.BlockSpec(memory_space=pl.ANY)
HBM = pl.BlockSpec(memory_space=pltpu.HBM)
LIMIT = 24 * 1024 * 1024
F32 = jnp.float32
LONG = 20000000


def stage_masks(n):
    stages, low = [], 1
    while low < n:
        if low < 4 or low * 4 > n:
            stages.append([low])
            low *= 2
        else:
            stages.append([low, 2 * low, 3 * low])
            low *= 4
    return stages[::-1]


def swap(x, mask):
    n = lax.axis_size("obs")
    return lax.ppermute(x, "obs", [(i, i ^ mask) for i in range(n)])


def shift(masks, mask):
    return [m ^ mask for m in masks]


def call(kernel, ins, outs, scratch=(), flops=0, moved=0, pinned=False, aliases=()):
    return pl.pallas_call(
        kernel,
        input_output_aliases=dict(aliases),
        out_shape=[pltpu.VMEM(s, F32) if pinned and len(s) == 4 else jax.ShapeDtypeStruct(s, F32) for s in outs],
        in_specs=ins,
        out_specs=[VMEM] * len(outs),
        scratch_shapes=list(scratch),
        compiler_params=pltpu.CompilerParams(vmem_limit_bytes=LIMIT),
        cost_estimate=pl.CostEstimate(flops=flops, bytes_accessed=moved, transcendentals=0),
    )


def pile_kernel(cuts, *refs):
    *arrays, _, pile_out = refs
    i = 0
    for array, (pitch, at, rows) in zip(arrays, cuts, strict=True):
        for start in range(0, array.shape[0], pitch):
            pile_out[i:i + rows, :] = array[start + at:start + at + rows, :]
            i += rows


def pile(arrays, cuts, after, cost=0):
    total = sum(a.shape[0] // pitch * rows for a, (pitch, _, rows) in zip(arrays, cuts, strict=True))
    cols = arrays[0].shape[1]
    return call(
        functools.partial(pile_kernel, cuts), [VMEM] * len(arrays) + [ANY], [(total, cols)],
        moved=max(8 * total * cols, cost), flops=cost * 300,
    )(*arrays, after)[0]


def lead_stages(x):
    masks, cut = [0], (x.shape[0], 0, x.shape[0])
    for stage in stage_masks(lax.axis_size("obs"))[:-3]:
        x = pile([x] + [swap(x, m) for m in stage], [cut] * (1 + len(stage)), x)
        masks = masks + [k for m in stage for k in shift(masks, m)]
    return x, masks


class Part:
    def __init__(self, array, masks, rest_masks=()):
        self.array, self.masks, self.rest_masks = array, tuple(masks), tuple(rest_masks)

    def swap(self, mask):
        return Part(swap(self.array, mask), shift(self.masks, mask), shift(self.rest_masks, mask))


def near_stages(first, second, wait=None):
    (pair,), (core,) = stage_masks(lax.axis_size("obs"))[-2:]
    parts = [first, first.swap(pair)]
    later = second(None)
    other = later.swap(pair)
    after, cost = (first.array, LONG) if wait is None else (wait(later.array), 0)
    whole = (other.array.shape[0], 0, other.array.shape[0])
    parts = parts + [later, Part(pile([other.array], [whole], after, cost), other.masks)]
    return parts + [p.swap(core) for p in parts]


def spread(x, rest, at, rows):
    size = x.shape[0]
    cut = (size, 0, size)
    x, masks = lead_stages(x)
    arrays, held, pitch = rest
    near, far, both = stage_masks(lax.axis_size("obs"))[-3]
    few = (pitch, at, rows)
    beyond, across = swap(x, far), swap(x, both)
    beside = swap(pile([x, arrays[2]], [cut, few], x), near)
    count = len(masks) * size
    first = pile(
        [x, beside, *arrays, beside],
        [(count, 0, count), (beside.shape[0], 0, count)] + [few] * 3 + [(beside.shape[0], count, beside.shape[0] - count)], x)
    first = Part(first, masks + shift(masks, near), held + shift(held, near) + shift(held, far) + shift(held, both))
    return near_stages(
        first, lambda _: Part(pile([beyond, across], [cut] * 2, x, LONG), shift(masks, far) + shift(masks, both)))


def spread_bundle(flux, bundle, own, ready, wait):
    pitch = bundle.shape[0]
    x, masks = lead_stages(bundle)
    near, far, both = stage_masks(lax.axis_size("obs"))[-3]
    cut = (pitch, 0, own)
    lone = flux if len(masks) == 1 else pile([x], [cut], x)
    across, beyond, beside = swap(lone, both), swap(x, far), swap(x, near)
    first = Part(pile([x, beside], [cut] * 2, ready), masks + shift(masks, near))
    parts = near_stages(first, lambda after: Part(
        pile([beyond, across], [cut, (own, 0, own)], ready), shift(masks, far) + shift(masks, both)), wait)
    return parts, ((x, beside, beyond), masks, pitch)


def bundle_kernel(ids, me, flux, prior, precision, bundle_out, want_out, prior_in, tile_ids, sem):
    each, blocks = tile_ids.shape
    count = blocks * each
    own, cols = flux.shape
    first = pltpu.make_async_copy(ids, tile_ids, sem.at[3])
    first.start()
    copies = [
        pltpu.make_async_copy(flux, bundle_out.at[pl.ds(0, own)], sem.at[0]),
        pltpu.make_async_copy(precision, bundle_out.at[pl.ds(2 * own + 8, own)], sem.at[1]),
        pltpu.make_async_copy(prior, prior_in, sem.at[2]),
    ]
    for c in copies:
        c.start()
    first.wait()
    lane = lax.broadcasted_iota(jnp.int32, (8, cols), 1) % count
    tall = lax.broadcasted_iota(jnp.int32, want_out.shape, 0)
    across = jnp.zeros((8, cols), jnp.int32)
    down = me[0] * own + tall - count
    for t in range(count):
        tile = tile_ids[t % each, t // each]
        across = jnp.where(lane == t, tile, across)
        down = jnp.where(tall == t, tile, down)
    bundle_out[2 * own:2 * own + 8, :] = across.astype(F32)
    want_out[...] = down.astype(F32)
    for c in copies:
        c.wait()
    bundle_out[own:2 * own, :] = bundle_out[2 * own + 8:, :] * (bundle_out[:own, :] - prior_in[...])


def prepare_kernel(counts, table_in, week_ids, observed, footprints, w_out, y_out, tiles_out,
                   week_weight, ids_in, y_in, sem):
    small = [
        pltpu.make_async_copy(week_ids, ids_in, sem.at[0]),
        pltpu.make_async_copy(table_in, week_weight, sem.at[2 + week_ids.shape[0] // 4]),
        pltpu.make_async_copy(observed, y_in, sem.at[1]),
    ]
    large = [
        pltpu.make_async_copy(footprints.at[pl.ds(i, 2)], tiles_out.at[pl.ds(i, 2)], sem.at[2 + i // 2])
        for i in range(0, footprints.shape[0] // 2, 2)
    ]
    for c in small:
        c.start()
    for c in large:
        c.start()
    for c in small:
        c.wait()
    blocks, rows = week_ids.shape
    ids = ids_in[...]
    table = jnp.zeros(ids.shape, F32)
    for week in range(week_weight.shape[0]):
        table = jnp.where(ids == week, week_weight[week], table)
    position = lax.broadcasted_iota(jnp.int32, ids.shape, 0) * rows + lax.broadcasted_iota(jnp.int32, ids.shape, 1)
    weights = jnp.where(position < counts[0], table, 0.0)
    fill = jnp.zeros((rows - blocks, rows), F32)
    w_out[...] = jnp.concatenate([weights, fill], axis=0).T
    y_out[...] = jnp.concatenate([y_in[...], fill], axis=0).T
    for c in large:
        c.wait()


def rest_kernel(footprints, tiles_in, after, tiles_out, done_out, sem):
    del tiles_in, after
    done_out[...] = jnp.zeros_like(done_out)
    half = footprints.shape[0] // 2
    copies = [
        pltpu.make_async_copy(footprints.at[pl.ds(i, 2)], tiles_out.at[pl.ds(i, 2)], sem.at[(i - half) // 2])
        for i in range(half, 2 * half, 2)
    ]
    for c in copies:
        c.start()
    for c in copies:
        c.wait()


def by_owner(me, pieces, rows, into):
    for m, ref, at in pieces:
        into[pl.ds(pl.multiple_of((me ^ m) * rows, 8), rows), :] = ref[at:at + rows, :]


def layout(shapes, refs, pitch, rest):
    pieces, others = [], []
    for (masks, rest_masks), ref in zip(shapes, refs, strict=True):
        pieces += [(m, ref, i * pitch) for i, m in enumerate(masks)]
        others += [(m, ref, len(masks) * pitch + i * rest) for i, m in enumerate(rest_masks)]
    return pieces, others


def forward_block(tiles, values, lane, b, minus):
    total = None
    for k, v in enumerate(values):
        part = tiles[b, k] * v
        total = part if total is None else total + part
    half = total.shape[1] // 2
    total = total[:, :half] + total[:, half:]
    if minus is not None:
        total = total - jnp.where(lane == b, minus, 0.0)
    return jnp.sum(total, axis=1, keepdims=True)


def transpose_block(tiles, weights, column, lane, b, terms_out):
    w = jnp.sum(jnp.where(lane == b, weights[...], 0.0), axis=1, keepdims=True)
    scaled = w * column
    each = tiles.shape[1]
    for k in range(each):
        terms_out[pl.ds(b * each + k, 1), :] = jnp.sum(tiles[b, k] * scaled, axis=0, keepdims=True)


def first_kernel(shapes, tile_ids, me, tiles, weights, observed, *refs):
    *parts, terms_out, departure_out, flux = refs
    blocks, each, tile_rows, _ = tiles.shape
    own = parts[0].shape[0] // len(shapes[0][0])
    by_owner(me[0], layout(shapes, parts, own, 0)[0], own, flux)
    lane = lax.broadcasted_iota(jnp.int32, (tile_rows, tile_rows), 1)
    departure_out[...] = jnp.zeros_like(departure_out)

    @pl.loop(0, blocks, unroll=4)
    def _(b):
        values = [flux[pl.ds(tile_ids[k, b], 1), :] for k in range(each)]
        depart = forward_block(tiles, values, lane, b, observed[...])
        departure_out[...] = jnp.where(lane == b, depart, departure_out[...])
        transpose_block(tiles, weights, depart, lane, b, terms_out)


def one_hot(order, names, want, piece, hot):
    lane = lax.broadcasted_iota(jnp.int32, (1, 128), 1)
    wanted = want[...]
    ids = {m: ref[at:at + 1, :128] for m, ref, at in names}
    for j in range(0, len(order), 2):
        pair = jnp.where(lane < piece, ids[order[j]], ids[order[j + 1]])
        hot[:, j * piece:(j + 2) * piece] = jnp.where(wanted == pair, 1.0, 0.0)


def sum_terms(pieces, piece, hot):
    block = jnp.concatenate([ref[at:at + piece, :] for _, ref, at in pieces], axis=0)
    marks = hot[...].astype(jnp.bfloat16)
    total = None
    for _ in range(3):
        part = block.astype(jnp.bfloat16)
        block = block - part.astype(F32)
        sums = jnp.dot(marks, part, preferred_element_type=F32)
        total = sums if total is None else total + sums
    return total


def sums_row(gradient, precision, weights, image, shape):
    square = jnp.sum(gradient * gradient)
    below = jnp.sum(precision * gradient * gradient) + jnp.sum(weights * image * image)
    lane = lax.broadcasted_iota(jnp.int32, shape, 1)
    return jnp.where(lane == 0, square, jnp.where(lane == 1, below, 0.0))


def second_kernel(shapes, tile_ids, me, tiles, weights, want, bundle, *refs):
    parts = refs[:len(shapes)]
    terms_out, gradient_out, image_out, hot, more = refs[len(shapes):]
    blocks, each, tile_rows, _ = tiles.shape
    count = blocks * each
    own = want.shape[0] - count
    pieces, others = layout(shapes, parts, count, own + 8)
    by_owner(me[0], others, own, more)
    one_hot([m for m, _, _ in pieces], [(m, ref, at + own) for m, ref, at in others], want, count, hot)
    lane = lax.broadcasted_iota(jnp.int32, (tile_rows, tile_rows), 1)
    image_out[...] = jnp.zeros_like(image_out)
    gradient_out[...] = sum_terms(pieces, count, hot)
    mine = gradient_out[count:, :] + bundle[own:2 * own, :]
    gradient_out[count:, :] = mine

    @pl.loop(0, blocks, unroll=4)
    def _(b):
        values = []
        for k in range(each):
            t = pl.ds(b * each + k, 1)
            value = gradient_out[t, :] + more[pl.ds(tile_ids[k, b], 1), :]
            gradient_out[t, :] = value
            values.append(value)
        image = forward_block(tiles, values, lane, b, None)
        image_out[...] = jnp.where(lane == b, image, image_out[...])
        transpose_block(tiles, weights, image, lane, b, terms_out)

    terms_out[count:, :] = sums_row(
        mine, bundle[2 * own + 8:3 * own + 8, :], weights[...], image_out[...], (8, terms_out.shape[1]))


def third_kernel(shapes, tile_ids, me, tiles, weights, want, bundle, hot, gradient, departure, image, *refs):
    parts = refs[:len(shapes)]
    sums_out, flux_out, gradient_out, departure_out, image_out, scale, second = refs[len(shapes):]
    blocks, each, tile_rows, _ = tiles.shape
    count = blocks * each
    own = want.shape[0] - count
    pieces, others = layout(shapes, parts, count + 8, own)
    by_owner(me[0], others, own, scale)
    lane = lax.broadcasted_iota(jnp.int32, (tile_rows, tile_rows), 1)
    sums = jnp.zeros((1, 128), F32)
    for _, ref, at in pieces:
        sums = sums + ref[at + count:at + count + 1, :128]
    step = sums[:, 0:1] / sums[:, 1:2]
    second[...] = sum_terms(pieces, count, hot)
    old = gradient[count:, :]
    precision = bundle[2 * own + 8:, :]
    mine = old - step * (second[count:, :] + precision * old)
    gradient_out[...] = mine
    flux_out[...] = bundle[:own, :] - step * old
    second[:count, :] = gradient[:count, :] - step * second[:count, :]

    def block(b, columns):
        values = []
        for k in range(each):
            t = pl.ds(b * each + k, 1)
            values.append(second[t, :] - step * scale[pl.ds(tile_ids[k, b], 1), :] * gradient[t, :])
        return jnp.where(lane == b, forward_block(tiles, values, lane, b, None), columns)

    columns = lax.fori_loop(0, blocks, block, jnp.zeros((tile_rows, tile_rows), F32), unroll=4)
    row = sums_row(mine, precision, weights[...], columns, (1, 128))
    sums_out[...] = jnp.broadcast_to(row[None], sums_out.shape)
    departure_out[...] = (departure[...] - step * image[...]).T[:blocks]
    image_out[...] = columns.T[:blocks]


def last_kernel(sums, flux, gradient, departure, image, flux_out, departure_out):
    total = jnp.sum(sums[...], axis=0)
    step = total[:, 0:1] / total[:, 1:2]
    flux_out[...] = flux[...] - step * gradient[...]
    departure_out[...] = departure[...] - step * image[...]


def body(footprints, tile_index, observed, week_ids, week_weight, counts, flux_start, flux_prior, prior_precision):
    n = lax.axis_size("obs")
    blocks, each, tile_rows, cols = footprints.shape
    own = flux_start.shape[0]
    count = blocks * each
    square = (tile_rows, tile_rows)
    place = (tile_index.T, lax.axis_index("obs").astype(jnp.int32)[None])

    def in_hbm(*arrays):
        return [pltpu.with_memory_space_constraint(x, pltpu.HBM) for x in arrays]

    pitch = 3 * own + 8
    bundle, want = call(
        bundle_kernel, [HBM, SMEM] + [HBM] * 3, [(pitch, cols), (count + own, 128)],
        [pltpu.VMEM((own, cols), F32), pltpu.SMEM((each, blocks), jnp.int32), pltpu.SemaphoreType.DMA((4,))],
        flops=10000, moved=12 * own * cols,
    )(*in_hbm(place[0]), place[1], *in_hbm(flux_start, flux_prior, prior_precision))
    weights, observed_t, tiles = call(
        prepare_kernel, [SMEM] + [HBM] * 4, [square, square, footprints.shape],
        [pltpu.SMEM(week_weight.shape, F32), pltpu.VMEM(week_ids.shape, jnp.int32), pltpu.VMEM(observed.shape, F32),
         pltpu.SemaphoreType.DMA((3 + blocks // 4,))],
        flops=10000, moved=8 * footprints.size, pinned=True,
    )(counts, *in_hbm(week_weight, week_ids, observed, footprints))

    staged = []

    def stage_rest(after):
        staged.extend(call(
            rest_kernel, [HBM, VMEM, ANY], [footprints.shape, (8, 128)], [pltpu.SemaphoreType.DMA((blocks // 4,))],
            moved=4 * footprints.size, pinned=True, aliases={1: 0},
        )(*in_hbm(footprints), pltpu.with_memory_space_constraint(tiles, pltpu.VMEM), after))
        return staged[1]

    parts, rest = spread_bundle(flux_start, bundle, own, weights, stage_rest)
    tiles = pltpu.with_memory_space_constraint(staged[0], pltpu.VMEM)

    def shapes():
        return [(p.masks, p.rest_masks) for p in parts]

    def arrays():
        return [p.array for p in parts]

    hot_shape = (count + own, n * count)
    whole = pltpu.VMEM((n * own, cols), F32)
    work = dict(flops=4 * footprints.size, moved=4 * footprints.size)
    terms, departure = call(
        functools.partial(first_kernel, shapes()), [SMEM] * 2 + [VMEM] * (3 + len(parts)),
        [(count, cols), square], [whole], **work,
    )(*place, tiles, weights, observed_t, *arrays())

    parts = spread(terms, rest, own, own + 8)
    terms, gradient, image, hot = call(
        functools.partial(second_kernel, shapes()), [SMEM] * 2 + [VMEM] * (4 + len(parts)),
        [(count + 8, cols), (count + own, cols), square, hot_shape], [whole], **work,
    )(*place, tiles, weights, want, bundle, *arrays())

    parts = spread(terms, rest, 2 * own + 8, own)
    sums, flux, gradient, departure, image = call(
        functools.partial(third_kernel, shapes()), [SMEM] * 2 + [VMEM] * (8 + len(parts)),
        [(n, 1, 128), (own, cols), (own, cols), (blocks, tile_rows), (blocks, tile_rows)],
        [whole, pltpu.VMEM((count + own, cols), F32)], **work,
    )(*place, tiles, weights, want, bundle, hot, gradient, departure, image, *arrays())

    sums = lax.all_to_all(sums, "obs", 0, 0)
    flux, departure = call(
        last_kernel, [VMEM] * 5, [(own, cols), (blocks, tile_rows)], flops=20000, moved=200000,
    )(sums, flux, gradient, departure, image)
    return flux, departure


def solution(mesh):
    rows = P(("groups", "obs"), None)
    return jax.shard_map(
        body,
        mesh=mesh,
        in_specs=(
            P(("groups", "obs"), None, None, None), rows, rows, rows,
            P("groups"), P(("groups", "obs")), rows, rows, rows,
        ),
        out_specs=(rows, rows),
        check_vma=False,
    )
```

```python
import functools

import jax
import jax.numpy as jnp
from jax import lax
from jax.experimental import pallas as pl
from jax.experimental.pallas import tpu as pltpu
from jax.sharding import PartitionSpec as P

VMEM = pl.BlockSpec(memory_space=pltpu.VMEM)
SMEM = pl.BlockSpec(memory_space=pltpu.SMEM)
ANY = pl.BlockSpec(memory_space=pl.ANY)
HBM = pl.BlockSpec(memory_space=pltpu.HBM)
LIMIT = 24 * 1024 * 1024
F32 = jnp.float32
LONG = 20000000


def stage_masks(n):
    stages, low = [], 1
    while low < n:
        if low < 4 or low * 4 > n:
            stages.append([low])
            low *= 2
        else:
            stages.append([low, 2 * low, 3 * low])
            low *= 4
    return stages[::-1]


def swap(x, mask):
    n = lax.axis_size("obs")
    return lax.ppermute(x, "obs", [(i, i ^ mask) for i in range(n)])


def shift(masks, mask):
    return [m ^ mask for m in masks]


def call(kernel, ins, outs, scratch=(), flops=0, moved=0, pinned=False):
    return pl.pallas_call(
        kernel,
        out_shape=[pltpu.VMEM(s, F32) if pinned and len(s) == 4 else jax.ShapeDtypeStruct(s, F32) for s in outs],
        in_specs=ins,
        out_specs=[VMEM] * len(outs),
        scratch_shapes=list(scratch),
        compiler_params=pltpu.CompilerParams(vmem_limit_bytes=LIMIT),
        cost_estimate=pl.CostEstimate(flops=flops, bytes_accessed=moved, transcendentals=0),
    )


def pile_kernel(cuts, *refs):
    *arrays, _, pile_out = refs
    i = 0
    for array, (pitch, at, rows) in zip(arrays, cuts, strict=True):
        for start in range(0, array.shape[0], pitch):
            pile_out[i:i + rows, :] = array[start + at:start + at + rows, :]
            i += rows


def pile(arrays, cuts, after, cost=0):
    total = sum(a.shape[0] // pitch * rows for a, (pitch, _, rows) in zip(arrays, cuts, strict=True))
    cols = arrays[0].shape[1]
    return call(
        functools.partial(pile_kernel, cuts), [VMEM] * len(arrays) + [ANY], [(total, cols)],
        moved=max(8 * total * cols, cost), flops=cost * 300,
    )(*arrays, after)[0]


def lead_stages(x):
    masks, cut = [0], (x.shape[0], 0, x.shape[0])
    for stage in stage_masks(lax.axis_size("obs"))[:-3]:
        x = pile([x] + [swap(x, m) for m in stage], [cut] * (1 + len(stage)), x)
        masks = masks + [k for m in stage for k in shift(masks, m)]
    return x, masks


class Part:
    def __init__(self, array, masks, rest_masks=()):
        self.array, self.masks, self.rest_masks = array, tuple(masks), tuple(rest_masks)

    def swap(self, mask):
        return Part(swap(self.array, mask), shift(self.masks, mask), shift(self.rest_masks, mask))


def near_stages(first, second, wide=None, cost=0):
    (pair,), (core,) = stage_masks(lax.axis_size("obs"))[-2:]
    other = second.swap(pair)
    whole = (other.array.shape[0], 0, other.array.shape[0])
    if cost:
        other = Part(pile([other.array], [whole], first.array, cost), other.masks)
    parts = [wide or first, first.swap(pair), second, other]
    return parts + [p.swap(core) for p in parts]


def spread(x, rest, at, rows):
    size = x.shape[0]
    cut = (size, 0, size)
    x, masks = lead_stages(x)
    bundle_far, mine, paired, held, pitch, own = rest
    near, far, both = stage_masks(lax.axis_size("obs"))[-3]
    (pair,) = stage_masks(lax.axis_size("obs"))[-2]
    beyond, across = swap(x, far), swap(x, both)
    beside = swap(pile([x, bundle_far], [cut, (pitch, own + at, rows)], x), near)
    count, extra = len(masks) * size, len(held) * rows
    first = Part(
        pile([x, beside, beside], [(count, 0, count), (count + extra, 0, count), (count + extra, count, extra)], x),
        masks + shift(masks, near), shift(held, both))
    second = Part(pile([beyond, across], [cut] * 2, x, LONG), shift(masks, far) + shift(masks, both))
    few = (pitch - own, at, rows)
    more = held + shift(held, near) + shift(held, far)
    wide = Part(
        pile([first.array, mine, paired], [(2 * count + extra, 0, 2 * count + extra), few, few], x),
        first.masks, list(first.rest_masks) + more + shift(more, pair))
    return near_stages(first, second, wide, LONG)


def spread_bundle(flux, bundle, own, ready):
    pitch = bundle.shape[0]
    x, masks = lead_stages(bundle)
    near, far, both = stage_masks(lax.axis_size("obs"))[-3]
    (pair,) = stage_masks(lax.axis_size("obs"))[-2]
    cut = (pitch, 0, own)
    lone = flux if len(masks) == 1 else pile([x], [cut], x)
    across, beyond, beside = swap(lone, both), swap(x, far), swap(x, near)
    first = Part(pile([x, beside], [cut] * 2, ready), masks + shift(masks, near))
    second = Part(pile([beyond, across], [cut, (own, 0, own)], ready), shift(masks, far) + shift(masks, both))
    parts = near_stages(first, second)
    mine = pile([x, beside, beyond], [(pitch, own, pitch - own)] * 3, second.array)
    return parts, (beyond, mine, swap(mine, pair), masks, pitch, own)


def bundle_kernel(ids, me, flux, prior, precision, bundle_out, want_out, prior_in, tile_ids, sem):
    each, blocks = tile_ids.shape
    count = blocks * each
    own, cols = flux.shape
    first = pltpu.make_async_copy(ids, tile_ids, sem.at[3])
    first.start()
    copies = [
        pltpu.make_async_copy(flux, bundle_out.at[pl.ds(0, own)], sem.at[0]),
        pltpu.make_async_copy(precision, bundle_out.at[pl.ds(2 * own + 8, own)], sem.at[1]),
        pltpu.make_async_copy(prior, prior_in, sem.at[2]),
    ]
    for c in copies:
        c.start()
    first.wait()
    lane = lax.broadcasted_iota(jnp.int32, (8, cols), 1) % count
    tall = lax.broadcasted_iota(jnp.int32, want_out.shape, 0)
    across = jnp.zeros((8, cols), jnp.int32)
    down = me[0] * own + tall - count
    for t in range(count):
        tile = tile_ids[t % each, t // each]
        across = jnp.where(lane == t, tile, across)
        down = jnp.where(tall == t, tile, down)
    bundle_out[2 * own:2 * own + 8, :] = across.astype(F32)
    want_out[...] = down.astype(F32)
    for c in copies:
        c.wait()
    bundle_out[own:2 * own, :] = bundle_out[2 * own + 8:, :] * (bundle_out[:own, :] - prior_in[...])


def prepare_kernel(counts, table_in, week_ids, observed, footprints, w_out, y_out, tiles_out,
                   week_weight, ids_in, y_in, sem):
    small = [
        pltpu.make_async_copy(week_ids, ids_in, sem.at[0]),
        pltpu.make_async_copy(table_in, week_weight, sem.at[2 + week_ids.shape[0] // 2]),
        pltpu.make_async_copy(observed, y_in, sem.at[1]),
    ]
    large = [
        pltpu.make_async_copy(footprints.at[pl.ds(i, 2)], tiles_out.at[pl.ds(i, 2)], sem.at[2 + i // 2])
        for i in range(0, footprints.shape[0], 2)
    ]
    for c in small:
        c.start()
    for c in large:
        c.start()
    for c in small:
        c.wait()
    blocks, rows = week_ids.shape
    ids = ids_in[...]
    table = jnp.zeros(ids.shape, F32)
    for week in range(week_weight.shape[0]):
        table = jnp.where(ids == week, week_weight[week], table)
    position = lax.broadcasted_iota(jnp.int32, ids.shape, 0) * rows + lax.broadcasted_iota(jnp.int32, ids.shape, 1)
    weights = jnp.where(position < counts[0], table, 0.0)
    fill = jnp.zeros((rows - blocks, rows), F32)
    w_out[...] = jnp.concatenate([weights, fill], axis=0).T
    y_out[...] = jnp.concatenate([y_in[...], fill], axis=0).T
    for c in large:
        c.wait()


def by_owner(me, pieces, rows, into):
    for m, ref, at in pieces:
        into[pl.ds(pl.multiple_of((me ^ m) * rows, 8), rows), :] = ref[at:at + rows, :]


def layout(shapes, refs, pitch, rest):
    pieces, others = [], []
    for (masks, rest_masks), ref in zip(shapes, refs, strict=True):
        pieces += [(m, ref, i * pitch) for i, m in enumerate(masks)]
        others += [(m, ref, len(masks) * pitch + i * rest) for i, m in enumerate(rest_masks)]
    return pieces, others


def forward_block(tiles, values, lane, b, minus):
    total = None
    for k, v in enumerate(values):
        part = tiles[b, k] * v
        total = part if total is None else total + part
    half = total.shape[1] // 2
    total = total[:, :half] + total[:, half:]
    if minus is not None:
        total = total - jnp.where(lane == b, minus, 0.0)
    return jnp.sum(total, axis=1, keepdims=True)


def transpose_block(tiles, weights, column, lane, b, terms_out):
    w = jnp.sum(jnp.where(lane == b, weights[...], 0.0), axis=1, keepdims=True)
    scaled = w * column
    each = tiles.shape[1]
    for k in range(each):
        terms_out[pl.ds(b * each + k, 1), :] = jnp.sum(tiles[b, k] * scaled, axis=0, keepdims=True)


def first_kernel(shapes, tile_ids, me, tiles, weights, observed, *refs):
    *parts, terms_out, departure_out, flux = refs
    blocks, each, tile_rows, _ = tiles.shape
    own = parts[0].shape[0] // len(shapes[0][0])
    by_owner(me[0], layout(shapes, parts, own, 0)[0], own, flux)
    lane = lax.broadcasted_iota(jnp.int32, (tile_rows, tile_rows), 1)

    def block(b, columns):
        values = [flux[pl.ds(tile_ids[k, b], 1), :] for k in range(each)]
        depart = forward_block(tiles, values, lane, b, observed[...])
        transpose_block(tiles, weights, depart, lane, b, terms_out)
        return jnp.where(lane == b, depart, columns)

    departure_out[...] = lax.fori_loop(0, blocks, block, jnp.zeros((tile_rows, tile_rows), F32), unroll=16)


def one_hot(order, names, want, piece, hot):
    lane = lax.broadcasted_iota(jnp.int32, (1, 128), 1)
    wanted = want[...]
    ids = {m: ref[at:at + 1, :128] for m, ref, at in names}
    for j in range(0, len(order), 2):
        pair = jnp.where(lane < piece, ids[order[j]], ids[order[j + 1]])
        hot[:, j * piece:(j + 2) * piece] = jnp.where(wanted == pair, 1.0, 0.0)


def sum_terms(pieces, piece, hot, start):
    block = jnp.concatenate([ref[at:at + piece, :] for _, ref, at in pieces], axis=0)
    marks = hot[:, start:start + len(pieces) * piece].astype(jnp.bfloat16)
    total = None
    for _ in range(3):
        part = block.astype(jnp.bfloat16)
        block = block - part.astype(F32)
        sums = jnp.dot(marks, part, preferred_element_type=F32)
        total = sums if total is None else total + sums
    return total


def sums_row(gradient, precision, weights, image, shape):
    square = jnp.sum(gradient * gradient)
    below = jnp.sum(precision * gradient * gradient) + jnp.sum(weights * image * image)
    lane = lax.broadcasted_iota(jnp.int32, shape, 1)
    return jnp.where(lane == 0, square, jnp.where(lane == 1, below, 0.0))


def early_kernel(shapes, pitch, rest, count, make_hot, me, want, *refs):
    parts, others = refs[:len(shapes)], refs[len(shapes):]
    pieces, more = layout(shapes, parts, pitch, rest)
    if make_hot:
        total_out, rows_out, hot = others
        marks = [(m, ref, at + rest - 8) for m, ref, at in more]
        late = [m for m, _, _ in more if m not in {p for p, _, _ in pieces}]
        one_hot([m for m, _, _ in pieces] + late, marks, want, count, hot)
    else:
        hot, total_out, rows_out = others
    by_owner(me[0], more, rows_out.shape[0] // len(more), rows_out)
    total_out[...] = sum_terms(pieces, count, hot, 0)


def second_kernel(shapes, tile_ids, me, tiles, weights, want, bundle, total, more, hot, *refs):
    parts = refs[:len(shapes)]
    terms_out, gradient_out, image_out = refs[len(shapes):]
    blocks, each, tile_rows, _ = tiles.shape
    count = blocks * each
    own = want.shape[0] - count
    pieces, _ = layout(shapes, parts, count, 0)
    lane = lax.broadcasted_iota(jnp.int32, (tile_rows, tile_rows), 1)
    gradient_out[...] = total[...] + sum_terms(pieces, count, hot, hot.shape[1] - len(pieces) * count)
    mine = gradient_out[count:, :] + bundle[own:2 * own, :]
    gradient_out[count:, :] = mine

    def block(b, columns):
        values = []
        for k in range(each):
            t = pl.ds(b * each + k, 1)
            value = gradient_out[t, :] + more[pl.ds(tile_ids[k, b], 1), :]
            gradient_out[t, :] = value
            values.append(value)
        image = forward_block(tiles, values, lane, b, None)
        transpose_block(tiles, weights, image, lane, b, terms_out)
        return jnp.where(lane == b, image, columns)

    columns = lax.fori_loop(0, blocks, block, jnp.zeros((tile_rows, tile_rows), F32), unroll=16)
    image_out[...] = columns
    terms_out[count:, :] = sums_row(
        mine, bundle[2 * own + 8:3 * own + 8, :], weights[...], columns, (8, terms_out.shape[1]))


def third_kernel(shapes, late_shapes, tile_ids, me, tiles, weights, want, bundle, total, scale, hot, gradient, departure,
                 image, *refs):
    parts, late = refs[:len(shapes)], refs[len(shapes):len(shapes) + len(late_shapes)]
    sums_out, flux_out, gradient_out, departure_out, image_out, second = refs[len(shapes) + len(late_shapes):]
    blocks, each, tile_rows, _ = tiles.shape
    count = blocks * each
    own = want.shape[0] - count
    lane = lax.broadcasted_iota(jnp.int32, (tile_rows, tile_rows), 1)
    late, _ = layout(late_shapes, late, count + 8, own)
    pieces = layout(shapes, parts, count + 8, own)[0] + late
    sums = jnp.zeros((1, 128), F32)
    for _, ref, at in pieces:
        sums = sums + ref[at + count:at + count + 1, :128]
    step = sums[:, 0:1] / sums[:, 1:2]
    second[...] = total[...] + sum_terms(late, count, hot, hot.shape[1] - len(late) * count)
    old = gradient[count:, :]
    precision = bundle[2 * own + 8:, :]
    mine = old - step * (second[count:, :] + precision * old)
    gradient_out[...] = mine
    flux_out[...] = bundle[:own, :] - step * old
    second[:count, :] = gradient[:count, :] - step * second[:count, :]

    def block(b, columns):
        values = []
        for k in range(each):
            t = pl.ds(b * each + k, 1)
            values.append(second[t, :] - step * scale[pl.ds(tile_ids[k, b], 1), :] * gradient[t, :])
        return jnp.where(lane == b, forward_block(tiles, values, lane, b, None), columns)

    columns = lax.fori_loop(0, blocks, block, jnp.zeros((tile_rows, tile_rows), F32), unroll=16)
    row = sums_row(mine, precision, weights[...], columns, (1, 128))
    sums_out[...] = jnp.broadcast_to(row[None], sums_out.shape)
    departure_out[...] = (departure[...] - step * image[...]).T[:blocks]
    image_out[...] = columns.T[:blocks]


def last_kernel(sums, flux, gradient, departure, image, flux_out, departure_out):
    total = jnp.sum(sums[...], axis=0)
    step = total[:, 0:1] / total[:, 1:2]
    flux_out[...] = flux[...] - step * gradient[...]
    departure_out[...] = departure[...] - step * image[...]


def body(footprints, tile_index, observed, week_ids, week_weight, counts, flux_start, flux_prior, prior_precision):
    n = lax.axis_size("obs")
    blocks, each, tile_rows, cols = footprints.shape
    own = flux_start.shape[0]
    count = blocks * each
    square = (tile_rows, tile_rows)
    place = (tile_index.T, lax.axis_index("obs").astype(jnp.int32)[None])

    def in_hbm(*arrays):
        return [pltpu.with_memory_space_constraint(x, pltpu.HBM) for x in arrays]

    pitch = 3 * own + 8
    bundle, want = call(
        bundle_kernel, [HBM, SMEM] + [HBM] * 3, [(pitch, cols), (count + own, 128)],
        [pltpu.VMEM((own, cols), F32), pltpu.SMEM((each, blocks), jnp.int32), pltpu.SemaphoreType.DMA((4,))],
        flops=10000, moved=12 * own * cols,
    )(*in_hbm(place[0]), place[1], *in_hbm(flux_start, flux_prior, prior_precision))
    weights, observed_t, tiles = call(
        prepare_kernel, [SMEM] + [HBM] * 4, [square, square, footprints.shape],
        [pltpu.SMEM(week_weight.shape, F32), pltpu.VMEM(week_ids.shape, jnp.int32), pltpu.VMEM(observed.shape, F32),
         pltpu.SemaphoreType.DMA((3 + blocks // 2,))],
        flops=10000, moved=8 * footprints.size, pinned=True,
    )(counts, *in_hbm(week_weight, week_ids, observed, footprints))

    parts, rest = spread_bundle(flux_start, bundle, own, weights)
    tiles = pltpu.with_memory_space_constraint(tiles, pltpu.VMEM)

    def shapes(parts):
        return [(p.masks, p.rest_masks) for p in parts]

    def arrays(parts):
        return [p.array for p in parts]

    def split(parts):
        return [p for i, p in enumerate(parts) if i % 4 != 3], parts[3::4]

    hot_shape = (count + own, n * count)
    whole = (n * own, cols)
    work = dict(flops=4 * footprints.size, moved=4 * footprints.size)
    terms, departure = call(
        functools.partial(first_kernel, shapes(parts)), [SMEM] * 2 + [VMEM] * (3 + len(parts)),
        [(count, cols), square], [pltpu.VMEM(whole, F32)], **work,
    )(*place, tiles, weights, observed_t, *arrays(parts))

    parts = spread(terms, rest, 0, own + 8)
    early, late = split(parts)
    total, more, hot = call(
        functools.partial(early_kernel, shapes(early), count, own + 8, count, True), [SMEM] + [VMEM] * (1 + len(early)),
        [(count + own, cols), whole, hot_shape], moved=4 * n * count * cols,
    )(place[1], want, *arrays(early))
    terms, gradient, image = call(
        functools.partial(second_kernel, shapes(late)), [SMEM] * 2 + [VMEM] * (7 + len(late)),
        [(count + 8, cols), (count + own, cols), square], **work,
    )(*place, tiles, weights, want, bundle, total, more, hot, *arrays(late))

    parts = spread(terms, rest, own + 8, own)
    early, late = split(parts)
    total, scale = call(
        functools.partial(early_kernel, shapes(early), count + 8, own, count, False),
        [SMEM] + [VMEM] * (2 + len(early)), [(count + own, cols), whole], moved=4 * n * count * cols,
    )(place[1], want, *arrays(early), hot)
    sums, flux, gradient, departure, image = call(
        functools.partial(third_kernel, shapes(early), shapes(late)),
        [SMEM] * 2 + [VMEM] * (10 + len(early) + len(late)),
        [(n, 1, 128), (own, cols), (own, cols), (blocks, tile_rows), (blocks, tile_rows)],
        [pltpu.VMEM((count + own, cols), F32)], **work,
    )(*place, tiles, weights, want, bundle, total, scale, hot, gradient, departure, image, *arrays(early), *arrays(late))

    sums = lax.all_to_all(sums, "obs", 0, 0)
    flux, departure = call(
        last_kernel, [VMEM] * 5, [(own, cols), (blocks, tile_rows)], flops=20000, moved=200000,
    )(sums, flux, gradient, departure, image)
    return flux, departure


def solution(mesh):
    rows = P(("groups", "obs"), None)
    return jax.shard_map(
        body,
        mesh=mesh,
        in_specs=(
            P(("groups", "obs"), None, None, None), rows, rows, rows,
            P("groups"), P(("groups", "obs")), rows, rows, rows,
        ),
        out_specs=(rows, rows),
        check_vma=False,
    )
```

```python
import functools

import jax
import jax.numpy as jnp
from jax import lax
from jax.experimental import pallas as pl
from jax.experimental.pallas import tpu as pltpu
from jax.sharding import PartitionSpec as P

VMEM = pl.BlockSpec(memory_space=pltpu.VMEM)
SMEM = pl.BlockSpec(memory_space=pltpu.SMEM)
ANY = pl.BlockSpec(memory_space=pl.ANY)
HBM = pl.BlockSpec(memory_space=pltpu.HBM)
LIMIT = 24 * 1024 * 1024
F32 = jnp.float32
LONG = 20000000


def stage_masks(n):
    stages, low = [], 1
    while low < n:
        if low < 4 or low * 4 > n:
            stages.append([low])
            low *= 2
        else:
            stages.append([low, 2 * low, 3 * low])
            low *= 4
    return stages[::-1]


def swap(x, mask):
    n = lax.axis_size("obs")
    return lax.ppermute(x, "obs", [(i, i ^ mask) for i in range(n)])


def shift(masks, mask):
    return [m ^ mask for m in masks]


def call(kernel, ins, outs, scratch=(), flops=0, moved=0, pinned=False):
    return pl.pallas_call(
        kernel,
        out_shape=[pltpu.VMEM(s, F32) if pinned and len(s) == 4 else jax.ShapeDtypeStruct(s, F32) for s in outs],
        in_specs=ins,
        out_specs=[VMEM] * len(outs),
        scratch_shapes=list(scratch),
        compiler_params=pltpu.CompilerParams(vmem_limit_bytes=LIMIT),
        cost_estimate=pl.CostEstimate(flops=flops, bytes_accessed=moved, transcendentals=0),
    )


def pile_kernel(cuts, *refs):
    *arrays, _, pile_out = refs
    i = 0
    for array, (pitch, at, rows) in zip(arrays, cuts, strict=True):
        for start in range(0, array.shape[0], pitch):
            pile_out[i:i + rows, :] = array[start + at:start + at + rows, :]
            i += rows


def pile(arrays, cuts, after, cost=0):
    total = sum(a.shape[0] // pitch * rows for a, (pitch, _, rows) in zip(arrays, cuts, strict=True))
    cols = arrays[0].shape[1]
    return call(
        functools.partial(pile_kernel, cuts), [VMEM] * len(arrays) + [ANY], [(total, cols)],
        moved=max(8 * total * cols, cost), flops=cost * 300,
    )(*arrays, after)[0]


def lead_stages(x):
    masks, cut = [0], (x.shape[0], 0, x.shape[0])
    for stage in stage_masks(lax.axis_size("obs"))[:-3]:
        x = pile([x] + [swap(x, m) for m in stage], [cut] * (1 + len(stage)), x)
        masks = masks + [k for m in stage for k in shift(masks, m)]
    return x, masks


class Part:
    def __init__(self, array, masks, rest_masks=()):
        self.array, self.masks, self.rest_masks = array, tuple(masks), tuple(rest_masks)

    def swap(self, mask):
        return Part(swap(self.array, mask), shift(self.masks, mask), shift(self.rest_masks, mask))


def near_stages(first, second, wide=None, cost=0):
    (pair,), (core,) = stage_masks(lax.axis_size("obs"))[-2:]
    other = second.swap(pair)
    whole = (other.array.shape[0], 0, other.array.shape[0])
    if cost:
        other = Part(pile([other.array], [whole], first.array, cost), other.masks)
    parts = [wide or first, first.swap(pair), second, other]
    return parts + [p.swap(core) for p in parts]


def spread(x, rest, at, rows):
    size = x.shape[0]
    cut = (size, 0, size)
    x, masks = lead_stages(x)
    bundle_far, mine, paired, held, pitch, own = rest
    near, far, both = stage_masks(lax.axis_size("obs"))[-3]
    (pair,) = stage_masks(lax.axis_size("obs"))[-2]
    beyond, across = swap(x, far), swap(x, both)
    beside = swap(pile([x, bundle_far], [cut, (pitch, own + at, rows)], x), near)
    count, extra = len(masks) * size, len(held) * rows
    first = Part(
        pile([x, beside, beside], [(count, 0, count), (count + extra, 0, count), (count + extra, count, extra)], paired),
        masks + shift(masks, near), shift(held, both))
    second = Part(pile([beyond, across], [cut] * 2, x, LONG), shift(masks, far) + shift(masks, both))
    few = (pitch - own, at, rows)
    more = held + shift(held, near) + shift(held, far)
    wide = Part(
        pile([first.array, mine, paired], [(2 * count + extra, 0, 2 * count + extra), few, few], x),
        first.masks, list(first.rest_masks) + more + shift(more, pair))
    return near_stages(first, second, wide, LONG)


def spread_bundle(flux, bundle, own, ready):
    pitch = bundle.shape[0]
    x, masks = lead_stages(bundle)
    near, far, both = stage_masks(lax.axis_size("obs"))[-3]
    (pair,) = stage_masks(lax.axis_size("obs"))[-2]
    cut = (pitch, 0, own)
    lone = flux if len(masks) == 1 else pile([x], [cut], x)
    across, beyond, beside = swap(lone, both), swap(x, far), swap(x, near)
    first = Part(pile([x, beside], [cut] * 2, ready), masks + shift(masks, near))
    second = Part(pile([beyond, across], [cut, (own, 0, own)], ready), shift(masks, far) + shift(masks, both))
    parts = near_stages(first, second)
    mine = pile([x, beside, beyond], [(pitch, own, pitch - own)] * 3, second.array)
    return parts, (beyond, mine, swap(mine, pair), masks, pitch, own)


def bundle_kernel(ids, me, flux, prior, precision, bundle_out, want_out, prior_in, tile_ids, sem):
    each, blocks = tile_ids.shape
    count = blocks * each
    own, cols = flux.shape
    first = pltpu.make_async_copy(ids, tile_ids, sem.at[3])
    first.start()
    copies = [
        pltpu.make_async_copy(flux, bundle_out.at[pl.ds(0, own)], sem.at[0]),
        pltpu.make_async_copy(precision, bundle_out.at[pl.ds(2 * own + 8, own)], sem.at[1]),
        pltpu.make_async_copy(prior, prior_in, sem.at[2]),
    ]
    for c in copies:
        c.start()
    first.wait()
    lane = lax.broadcasted_iota(jnp.int32, (8, cols), 1) % count
    tall = lax.broadcasted_iota(jnp.int32, want_out.shape, 0)
    across = jnp.zeros((8, cols), jnp.int32)
    down = me[0] * own + tall - count
    for t in range(count):
        tile = tile_ids[t % each, t // each]
        across = jnp.where(lane == t, tile, across)
        down = jnp.where(tall == t, tile, down)
    bundle_out[2 * own:2 * own + 8, :] = across.astype(F32)
    want_out[...] = down.astype(F32)
    for c in copies:
        c.wait()
    bundle_out[own:2 * own, :] = bundle_out[2 * own + 8:, :] * (bundle_out[:own, :] - prior_in[...])


def prepare_kernel(counts, table_in, week_ids, observed, footprints, w_out, y_out, tiles_out,
                   week_weight, ids_in, y_in, sem):
    small = [
        pltpu.make_async_copy(week_ids, ids_in, sem.at[0]),
        pltpu.make_async_copy(table_in, week_weight, sem.at[2 + week_ids.shape[0] // 2]),
        pltpu.make_async_copy(observed, y_in, sem.at[1]),
    ]
    large = [
        pltpu.make_async_copy(footprints.at[pl.ds(i, 2)], tiles_out.at[pl.ds(i, 2)], sem.at[2 + i // 2])
        for i in range(0, footprints.shape[0], 2)
    ]
    for c in small:
        c.start()
    for c in large:
        c.start()
    for c in small:
        c.wait()
    blocks, rows = week_ids.shape
    ids = ids_in[...]
    table = jnp.zeros(ids.shape, F32)
    for week in range(week_weight.shape[0]):
        table = jnp.where(ids == week, week_weight[week], table)
    position = lax.broadcasted_iota(jnp.int32, ids.shape, 0) * rows + lax.broadcasted_iota(jnp.int32, ids.shape, 1)
    weights = jnp.where(position < counts[0], table, 0.0)
    fill = jnp.zeros((rows - blocks, rows), F32)
    w_out[...] = jnp.concatenate([weights, fill], axis=0).T
    y_out[...] = jnp.concatenate([y_in[...], fill], axis=0).T
    for c in large:
        c.wait()


def by_owner(me, pieces, rows, into):
    for m, ref, at in pieces:
        into[pl.ds(pl.multiple_of((me ^ m) * rows, 8), rows), :] = ref[at:at + rows, :]


def layout(shapes, refs, pitch, rest):
    pieces, others = [], []
    for (masks, rest_masks), ref in zip(shapes, refs, strict=True):
        pieces += [(m, ref, i * pitch) for i, m in enumerate(masks)]
        others += [(m, ref, len(masks) * pitch + i * rest) for i, m in enumerate(rest_masks)]
    return pieces, others


def forward_block(tiles, values, lane, b, minus):
    total = None
    for k, v in enumerate(values):
        part = tiles[b, k] * v
        total = part if total is None else total + part
    half = total.shape[1] // 2
    total = total[:, :half] + total[:, half:]
    if minus is not None:
        total = total - jnp.where(lane == b, minus, 0.0)
    return jnp.sum(total, axis=1, keepdims=True)


def transpose_block(tiles, weights, column, lane, b, terms_out):
    w = jnp.sum(jnp.where(lane == b, weights[...], 0.0), axis=1, keepdims=True)
    scaled = w * column
    each = tiles.shape[1]
    for k in range(each):
        terms_out[pl.ds(b * each + k, 1), :] = jnp.sum(tiles[b, k] * scaled, axis=0, keepdims=True)


def first_kernel(shapes, ids, me, tiles, weights, observed, *refs):
    *parts, terms_out, departure_out, flux, tile_ids, sem = refs
    copy = pltpu.make_async_copy(ids, tile_ids, sem)
    copy.start()
    blocks, each, tile_rows, _ = tiles.shape
    own = parts[0].shape[0] // len(shapes[0][0])
    by_owner(me[0], layout(shapes, parts, own, 0)[0], own, flux)
    copy.wait()
    lane = lax.broadcasted_iota(jnp.int32, (tile_rows, tile_rows), 1)

    def block(b, columns):
        values = [flux[pl.ds(tile_ids[k, b], 1), :] for k in range(each)]
        depart = forward_block(tiles, values, lane, b, observed[...])
        transpose_block(tiles, weights, depart, lane, b, terms_out)
        return jnp.where(lane == b, depart, columns)

    departure_out[...] = lax.fori_loop(0, blocks, block, jnp.zeros((tile_rows, tile_rows), F32), unroll=16)


def one_hot(order, names, want, piece, hot):
    lane = lax.broadcasted_iota(jnp.int32, (1, 128), 1)
    wanted = want[...]
    ids = {m: ref[at:at + 1, :128] for m, ref, at in names}
    for j in range(0, len(order), 2):
        pair = jnp.where(lane < piece, ids[order[j]], ids[order[j + 1]])
        hot[:, j * piece:(j + 2) * piece] = jnp.where(wanted == pair, 1.0, 0.0)


def sum_terms(pieces, piece, hot, start):
    block = jnp.concatenate([ref[at:at + piece, :] for _, ref, at in pieces], axis=0)
    marks = hot[:, start:start + len(pieces) * piece].astype(jnp.bfloat16)
    total = None
    for _ in range(3):
        part = block.astype(jnp.bfloat16)
        block = block - part.astype(F32)
        sums = jnp.dot(marks, part, preferred_element_type=F32)
        total = sums if total is None else total + sums
    return total


def sums_row(gradient, precision, weights, image, shape):
    square = jnp.sum(gradient * gradient)
    below = jnp.sum(precision * gradient * gradient) + jnp.sum(weights * image * image)
    lane = lax.broadcasted_iota(jnp.int32, shape, 1)
    return jnp.where(lane == 0, square, jnp.where(lane == 1, below, 0.0))


def early_kernel(shapes, pitch, rest, count, make_hot, me, want, *refs):
    parts, others = refs[:len(shapes)], refs[len(shapes):]
    pieces, more = layout(shapes, parts, pitch, rest)
    if make_hot:
        total_out, rows_out, hot = others
        marks = [(m, ref, at + rest - 8) for m, ref, at in more]
        late = [m for m, _, _ in more if m not in {p for p, _, _ in pieces}]
        one_hot([m for m, _, _ in pieces] + late, marks, want, count, hot)
    else:
        hot, total_out, rows_out = others
    by_owner(me[0], more, rows_out.shape[0] // len(more), rows_out)
    total_out[...] = sum_terms(pieces, count, hot, 0)


def second_kernel(shapes, ids, me, tiles, weights, want, bundle, total, more, hot, *refs):
    parts = refs[:len(shapes)]
    terms_out, gradient_out, image_out, tile_ids, sem = refs[len(shapes):]
    copy = pltpu.make_async_copy(ids, tile_ids, sem)
    copy.start()
    blocks, each, tile_rows, _ = tiles.shape
    count = blocks * each
    own = want.shape[0] - count
    pieces, _ = layout(shapes, parts, count, 0)
    lane = lax.broadcasted_iota(jnp.int32, (tile_rows, tile_rows), 1)
    gradient_out[...] = total[...] + sum_terms(pieces, count, hot, hot.shape[1] - len(pieces) * count)
    copy.wait()
    mine = gradient_out[count:, :] + bundle[own:2 * own, :]
    gradient_out[count:, :] = mine

    def block(b, columns):
        values = []
        for k in range(each):
            t = pl.ds(b * each + k, 1)
            value = gradient_out[t, :] + more[pl.ds(tile_ids[k, b], 1), :]
            gradient_out[t, :] = value
            values.append(value)
        image = forward_block(tiles, values, lane, b, None)
        transpose_block(tiles, weights, image, lane, b, terms_out)
        return jnp.where(lane == b, image, columns)

    columns = lax.fori_loop(0, blocks, block, jnp.zeros((tile_rows, tile_rows), F32), unroll=16)
    image_out[...] = columns
    terms_out[count:, :] = sums_row(
        mine, bundle[2 * own + 8:3 * own + 8, :], weights[...], columns, (8, terms_out.shape[1]))


def third_kernel(shapes, late_shapes, ids, me, tiles, weights, want, bundle, total, scale, hot, gradient, departure,
                 image, *refs):
    parts, late = refs[:len(shapes)], refs[len(shapes):len(shapes) + len(late_shapes)]
    sums_out, flux_out, gradient_out, departure_out, image_out, second, tile_ids, sem = refs[len(shapes) + len(late_shapes):]
    copy = pltpu.make_async_copy(ids, tile_ids, sem)
    copy.start()
    blocks, each, tile_rows, _ = tiles.shape
    count = blocks * each
    own = want.shape[0] - count
    lane = lax.broadcasted_iota(jnp.int32, (tile_rows, tile_rows), 1)
    late, _ = layout(late_shapes, late, count + 8, own)
    pieces = layout(shapes, parts, count + 8, own)[0] + late
    sums = jnp.zeros((1, 128), F32)
    for _, ref, at in pieces:
        sums = sums + ref[at + count:at + count + 1, :128]
    step = sums[:, 0:1] / sums[:, 1:2]
    second[...] = total[...] + sum_terms(late, count, hot, hot.shape[1] - len(late) * count)
    copy.wait()
    old = gradient[count:, :]
    precision = bundle[2 * own + 8:, :]
    mine = old - step * (second[count:, :] + precision * old)
    gradient_out[...] = mine
    flux_out[...] = bundle[:own, :] - step * old
    second[:count, :] = gradient[:count, :] - step * second[:count, :]

    def block(b, columns):
        values = []
        for k in range(each):
            t = pl.ds(b * each + k, 1)
            values.append(second[t, :] - step * scale[pl.ds(tile_ids[k, b], 1), :] * gradient[t, :])
        return jnp.where(lane == b, forward_block(tiles, values, lane, b, None), columns)

    columns = lax.fori_loop(0, blocks, block, jnp.zeros((tile_rows, tile_rows), F32), unroll=16)
    row = sums_row(mine, precision, weights[...], columns, (1, 128))
    sums_out[...] = jnp.broadcast_to(row[None], sums_out.shape)
    departure_out[...] = (departure[...] - step * image[...]).T[:blocks]
    image_out[...] = columns.T[:blocks]


def last_kernel(sums, flux, gradient, departure, image, flux_out, departure_out):
    total = jnp.sum(sums[...], axis=0)
    step = total[:, 0:1] / total[:, 1:2]
    flux_out[...] = flux[...] - step * gradient[...]
    departure_out[...] = departure[...] - step * image[...]


def body(footprints, tile_index, observed, week_ids, week_weight, counts, flux_start, flux_prior, prior_precision):
    n = lax.axis_size("obs")
    blocks, each, tile_rows, cols = footprints.shape
    own = flux_start.shape[0]
    count = blocks * each
    square = (tile_rows, tile_rows)
    place = (tile_index.T, lax.axis_index("obs").astype(jnp.int32)[None])

    def in_hbm(*arrays):
        return [pltpu.with_memory_space_constraint(x, pltpu.HBM) for x in arrays]

    pitch = 3 * own + 8
    bundle, want = call(
        bundle_kernel, [HBM, SMEM] + [HBM] * 3, [(pitch, cols), (count + own, 128)],
        [pltpu.VMEM((own, cols), F32), pltpu.SMEM((each, blocks), jnp.int32), pltpu.SemaphoreType.DMA((4,))],
        flops=10000, moved=12 * own * cols,
    )(*in_hbm(place[0]), place[1], *in_hbm(flux_start, flux_prior, prior_precision))
    weights, observed_t, tiles = call(
        prepare_kernel, [SMEM] + [HBM] * 4, [square, square, footprints.shape],
        [pltpu.SMEM(week_weight.shape, F32), pltpu.VMEM(week_ids.shape, jnp.int32), pltpu.VMEM(observed.shape, F32),
         pltpu.SemaphoreType.DMA((3 + blocks // 2,))],
        flops=10000, moved=8 * footprints.size, pinned=True,
    )(counts, *in_hbm(week_weight, week_ids, observed, footprints))

    parts, rest = spread_bundle(flux_start, bundle, own, weights)
    tiles = pltpu.with_memory_space_constraint(tiles, pltpu.VMEM)

    def shapes(parts):
        return [(p.masks, p.rest_masks) for p in parts]

    def arrays(parts):
        return [p.array for p in parts]

    def split(parts):
        return [p for i, p in enumerate(parts) if i % 4 != 3], parts[3::4]

    ids_scratch = [pltpu.SMEM((each, blocks), jnp.int32), pltpu.SemaphoreType.DMA]
    hot_shape = (count + own, n * count)
    whole = (n * own, cols)
    work = dict(flops=4 * footprints.size, moved=4 * footprints.size)
    terms, departure = call(
        functools.partial(first_kernel, shapes(parts)), [VMEM, SMEM] + [VMEM] * (3 + len(parts)),
        [(count, cols), square], [pltpu.VMEM(whole, F32), *ids_scratch], **work,
    )(*place, tiles, weights, observed_t, *arrays(parts))

    parts = spread(terms, rest, 0, own + 8)
    early, late = split(parts)
    total, more, hot = call(
        functools.partial(early_kernel, shapes(early), count, own + 8, count, True), [SMEM] + [VMEM] * (1 + len(early)),
        [(count + own, cols), whole, hot_shape], moved=4 * n * count * cols,
    )(place[1], want, *arrays(early))
    terms, gradient, image = call(
        functools.partial(second_kernel, shapes(late)), [VMEM, SMEM] + [VMEM] * (7 + len(late)),
        [(count + 8, cols), (count + own, cols), square], ids_scratch, **work,
    )(*place, tiles, weights, want, bundle, total, more, hot, *arrays(late))

    parts = spread(terms, rest, own + 8, own)
    early, late = split(parts)
    total, scale = call(
        functools.partial(early_kernel, shapes(early), count + 8, own, count, False),
        [SMEM] + [VMEM] * (2 + len(early)), [(count + own, cols), whole], moved=4 * n * count * cols,
    )(place[1], want, *arrays(early), hot)
    sums, flux, gradient, departure, image = call(
        functools.partial(third_kernel, shapes(early), shapes(late)),
        [VMEM, SMEM] + [VMEM] * (10 + len(early) + len(late)),
        [(n, 1, 128), (own, cols), (own, cols), (blocks, tile_rows), (blocks, tile_rows)],
        [pltpu.VMEM((count + own, cols), F32), *ids_scratch], **work,
    )(*place, tiles, weights, want, bundle, total, scale, hot, gradient, departure, image, *arrays(early), *arrays(late))

    sums = lax.all_to_all(sums, "obs", 0, 0)
    flux, departure = call(
        last_kernel, [VMEM] * 5, [(own, cols), (blocks, tile_rows)], flops=20000, moved=200000,
    )(sums, flux, gradient, departure, image)
    return flux, departure


def solution(mesh):
    rows = P(("groups", "obs"), None)
    return jax.shard_map(
        body,
        mesh=mesh,
        in_specs=(
            P(("groups", "obs"), None, None, None), rows, rows, rows,
            P("groups"), P(("groups", "obs")), rows, rows, rows,
        ),
        out_specs=(rows, rows),
        check_vma=False,
    )
```

```python
import functools

import jax
import jax.numpy as jnp
from jax import lax
from jax.experimental import pallas as pl
from jax.experimental.pallas import tpu as pltpu
from jax.sharding import PartitionSpec as P

VMEM = pl.BlockSpec(memory_space=pltpu.VMEM)
SMEM = pl.BlockSpec(memory_space=pltpu.SMEM)
ANY = pl.BlockSpec(memory_space=pl.ANY)
HBM = pl.BlockSpec(memory_space=pltpu.HBM)
LIMIT = 24 * 1024 * 1024
F32 = jnp.float32
LONG = 20000000


def stage_masks(n):
    stages, low = [], 1
    while low < n:
        if low < 4 or low * 4 > n:
            stages.append([low])
            low *= 2
        else:
            stages.append([low, 2 * low, 3 * low])
            low *= 4
    return stages[::-1]


def swap(x, mask):
    n = lax.axis_size("obs")
    return lax.ppermute(x, "obs", [(i, i ^ mask) for i in range(n)])


def shift(masks, mask):
    return [m ^ mask for m in masks]


def call(kernel, ins, outs, scratch=(), flops=0, moved=0, pinned=False):
    return pl.pallas_call(
        kernel,
        out_shape=[pltpu.VMEM(s, F32) if pinned and len(s) == 4 else jax.ShapeDtypeStruct(s, F32) for s in outs],
        in_specs=ins,
        out_specs=[VMEM] * len(outs),
        scratch_shapes=list(scratch),
        compiler_params=pltpu.CompilerParams(vmem_limit_bytes=LIMIT),
        cost_estimate=pl.CostEstimate(flops=flops, bytes_accessed=moved, transcendentals=0),
    )


def pile_kernel(cuts, *refs):
    *arrays, _, pile_out = refs
    i = 0
    for array, (pitch, at, rows) in zip(arrays, cuts, strict=True):
        for start in range(0, array.shape[0], pitch):
            pile_out[i:i + rows, :] = array[start + at:start + at + rows, :]
            i += rows


def pile(arrays, cuts, after, cost=0):
    total = sum(a.shape[0] // pitch * rows for a, (pitch, _, rows) in zip(arrays, cuts, strict=True))
    cols = arrays[0].shape[1]
    return call(
        functools.partial(pile_kernel, cuts), [VMEM] * len(arrays) + [ANY], [(total, cols)],
        moved=max(8 * total * cols, cost), flops=cost * 300,
    )(*arrays, after)[0]


def lead_stages(x):
    masks, cut = [0], (x.shape[0], 0, x.shape[0])
    for stage in stage_masks(lax.axis_size("obs"))[:-3]:
        x = pile([x] + [swap(x, m) for m in stage], [cut] * (1 + len(stage)), x)
        masks = masks + [k for m in stage for k in shift(masks, m)]
    return x, masks


class Part:
    def __init__(self, array, masks, rest_masks=()):
        self.array, self.masks, self.rest_masks = array, tuple(masks), tuple(rest_masks)

    def swap(self, mask):
        return Part(swap(self.array, mask), shift(self.masks, mask), shift(self.rest_masks, mask))


def near_stages(first, second, wide=None, cost=0):
    (pair,), (core,) = stage_masks(lax.axis_size("obs"))[-2:]
    other = second.swap(pair)
    whole = (other.array.shape[0], 0, other.array.shape[0])
    if cost:
        other = Part(pile([other.array], [whole], first.array, cost), other.masks)
    parts = [wide or first, first.swap(pair), second, other]
    return parts + [p.swap(core) for p in parts]


def spread(x, rest, at, rows):
    size = x.shape[0]
    cut = (size, 0, size)
    x, masks = lead_stages(x)
    bundle_far, mine, paired, held, pitch, own = rest
    near, far, both = stage_masks(lax.axis_size("obs"))[-3]
    (pair,) = stage_masks(lax.axis_size("obs"))[-2]
    beyond, across = swap(x, far), swap(x, both)
    beside = swap(pile([x, bundle_far], [cut, (pitch, own + at, rows)], x), near)
    count, extra = len(masks) * size, len(held) * rows
    first = Part(
        pile([x, beside, beside], [(count, 0, count), (count + extra, 0, count), (count + extra, count, extra)], paired),
        masks + shift(masks, near), shift(held, both))
    second = Part(pile([beyond, across], [cut] * 2, x), shift(masks, far) + shift(masks, both))
    few = (pitch - own, at, rows)
    more = held + shift(held, near) + shift(held, far)
    wide = Part(
        pile([first.array, mine, paired], [(2 * count + extra, 0, 2 * count + extra), few, few], x),
        first.masks, list(first.rest_masks) + more + shift(more, pair))
    return near_stages(first, second, wide, LONG)


def spread_bundle(flux, bundle, own, ready):
    pitch = bundle.shape[0]
    x, masks = lead_stages(bundle)
    near, far, both = stage_masks(lax.axis_size("obs"))[-3]
    (pair,) = stage_masks(lax.axis_size("obs"))[-2]
    cut = (pitch, 0, own)
    lone = flux if len(masks) == 1 else pile([x], [cut], x)
    across, beyond, beside = swap(lone, both), swap(x, far), swap(x, near)
    first = Part(pile([x, beside], [cut] * 2, ready), masks + shift(masks, near))
    second = Part(pile([beyond, across], [cut, (own, 0, own)], ready), shift(masks, far) + shift(masks, both))
    parts = near_stages(first, second)
    mine = pile([x, beside, beyond], [(pitch, own, pitch - own)] * 3, second.array)
    return parts, (beyond, mine, swap(mine, pair), masks, pitch, own)


def bundle_kernel(ids, me, flux, prior, precision, bundle_out, want_out, prior_in, tile_ids, sem):
    each, blocks = tile_ids.shape
    count = blocks * each
    own, cols = flux.shape
    first = pltpu.make_async_copy(ids, tile_ids, sem.at[3])
    first.start()
    copies = [
        pltpu.make_async_copy(flux, bundle_out.at[pl.ds(0, own)], sem.at[0]),
        pltpu.make_async_copy(precision, bundle_out.at[pl.ds(2 * own + 8, own)], sem.at[1]),
        pltpu.make_async_copy(prior, prior_in, sem.at[2]),
    ]
    for c in copies:
        c.start()
    first.wait()
    lane = lax.broadcasted_iota(jnp.int32, (8, cols), 1) % count
    tall = lax.broadcasted_iota(jnp.int32, want_out.shape, 0)
    across = jnp.zeros((8, cols), jnp.int32)
    down = me[0] * own + tall - count
    for t in range(count):
        tile = tile_ids[t % each, t // each]
        across = jnp.where(lane == t, tile, across)
        down = jnp.where(tall == t, tile, down)
    bundle_out[2 * own:2 * own + 8, :] = across.astype(F32)
    want_out[...] = down.astype(F32)
    for c in copies:
        c.wait()
    bundle_out[own:2 * own, :] = bundle_out[2 * own + 8:, :] * (bundle_out[:own, :] - prior_in[...])


def prepare_kernel(counts, table_in, week_ids, observed, footprints, w_out, y_out, tiles_out,
                   week_weight, ids_in, y_in, sem):
    small = [
        pltpu.make_async_copy(week_ids, ids_in, sem.at[0]),
        pltpu.make_async_copy(table_in, week_weight, sem.at[2 + week_ids.shape[0] // 2]),
        pltpu.make_async_copy(observed, y_in, sem.at[1]),
    ]
    large = [
        pltpu.make_async_copy(footprints.at[pl.ds(i, 2)], tiles_out.at[pl.ds(i, 2)], sem.at[2 + i // 2])
        for i in range(0, footprints.shape[0], 2)
    ]
    for c in large:
        c.start()
    for c in small:
        c.start()
    for c in small:
        c.wait()
    blocks, rows = week_ids.shape
    ids = ids_in[...]
    table = jnp.zeros(ids.shape, F32)
    for week in range(week_weight.shape[0]):
        table = jnp.where(ids == week, week_weight[week], table)
    position = lax.broadcasted_iota(jnp.int32, ids.shape, 0) * rows + lax.broadcasted_iota(jnp.int32, ids.shape, 1)
    weights = jnp.where(position < counts[0], table, 0.0)
    fill = jnp.zeros((rows - blocks, rows), F32)
    w_out[...] = jnp.concatenate([weights, fill], axis=0).T
    y_out[...] = jnp.concatenate([y_in[...], fill], axis=0).T
    for c in large:
        c.wait()


def by_owner(me, pieces, rows, into):
    for m, ref, at in pieces:
        into[pl.ds(pl.multiple_of((me ^ m) * rows, 8), rows), :] = ref[at:at + rows, :]


def layout(shapes, refs, pitch, rest):
    pieces, others = [], []
    for (masks, rest_masks), ref in zip(shapes, refs, strict=True):
        pieces += [(m, ref, i * pitch) for i, m in enumerate(masks)]
        others += [(m, ref, len(masks) * pitch + i * rest) for i, m in enumerate(rest_masks)]
    return pieces, others


def forward_block(tiles, values, lane, b, minus):
    total = None
    for k, v in enumerate(values):
        part = tiles[b, k] * v
        total = part if total is None else total + part
    half = total.shape[1] // 2
    total = total[:, :half] + total[:, half:]
    if minus is not None:
        total = total - jnp.where(lane == b, minus, 0.0)
    return jnp.sum(total, axis=1, keepdims=True)


def transpose_block(tiles, weights, column, lane, b, terms_out):
    w = jnp.sum(jnp.where(lane == b, weights[...], 0.0), axis=1, keepdims=True)
    scaled = w * column
    each = tiles.shape[1]
    for k in range(each):
        terms_out[pl.ds(b * each + k, 1), :] = jnp.sum(tiles[b, k] * scaled, axis=0, keepdims=True)


def first_kernel(shapes, ids, me, tiles, weights, observed, *refs):
    *parts, terms_out, departure_out, flux, tile_ids, sem = refs
    copy = pltpu.make_async_copy(ids, tile_ids, sem)
    copy.start()
    blocks, each, tile_rows, _ = tiles.shape
    own = parts[0].shape[0] // len(shapes[0][0])
    by_owner(me[0], layout(shapes, parts, own, 0)[0], own, flux)
    copy.wait()
    lane = lax.broadcasted_iota(jnp.int32, (tile_rows, tile_rows), 1)

    def block(b, columns):
        values = [flux[pl.ds(tile_ids[k, b], 1), :] for k in range(each)]
        depart = forward_block(tiles, values, lane, b, observed[...])
        transpose_block(tiles, weights, depart, lane, b, terms_out)
        return jnp.where(lane == b, depart, columns)

    departure_out[...] = lax.fori_loop(0, blocks, block, jnp.zeros((tile_rows, tile_rows), F32), unroll=16)


def one_hot(order, names, want, piece, hot):
    lane = lax.broadcasted_iota(jnp.int32, (1, 128), 1)
    wanted = want[...]
    ids = {m: ref[at:at + 1, :128] for m, ref, at in names}
    for j in range(0, len(order), 2):
        pair = jnp.where(lane < piece, ids[order[j]], ids[order[j + 1]])
        hot[:, j * piece:(j + 2) * piece] = jnp.where(wanted == pair, 1.0, 0.0)


def sum_terms(pieces, piece, hot, start):
    block = jnp.concatenate([ref[at:at + piece, :] for _, ref, at in pieces], axis=0)
    marks = hot[:, start:start + len(pieces) * piece].astype(jnp.bfloat16)
    total = None
    for _ in range(3):
        part = block.astype(jnp.bfloat16)
        block = block - part.astype(F32)
        sums = jnp.dot(marks, part, preferred_element_type=F32)
        total = sums if total is None else total + sums
    return total


def sums_row(gradient, precision, weights, image, shape):
    square = jnp.sum(gradient * gradient)
    below = jnp.sum(precision * gradient * gradient) + jnp.sum(weights * image * image)
    lane = lax.broadcasted_iota(jnp.int32, shape, 1)
    return jnp.where(lane == 0, square, jnp.where(lane == 1, below, 0.0))


def early_kernel(shapes, pitch, rest, count, make_hot, me, want, *refs):
    parts, others = refs[:len(shapes)], refs[len(shapes):]
    pieces, more = layout(shapes, parts, pitch, rest)
    if make_hot:
        total_out, rows_out, hot = others
        marks = [(m, ref, at + rest - 8) for m, ref, at in more]
        late = [m for m, _, _ in more if m not in {p for p, _, _ in pieces}]
        one_hot([m for m, _, _ in pieces] + late, marks, want, count, hot)
    else:
        hot, total_out, rows_out = others
    by_owner(me[0], more, rows_out.shape[0] // len(more), rows_out)
    total_out[...] = sum_terms(pieces, count, hot, 0)


def second_kernel(shapes, ids, me, tiles, weights, want, bundle, total, more, hot, *refs):
    parts = refs[:len(shapes)]
    terms_out, gradient_out, image_out, tile_ids, sem = refs[len(shapes):]
    copy = pltpu.make_async_copy(ids, tile_ids, sem)
    copy.start()
    blocks, each, tile_rows, _ = tiles.shape
    count = blocks * each
    own = want.shape[0] - count
    pieces, _ = layout(shapes, parts, count, 0)
    lane = lax.broadcasted_iota(jnp.int32, (tile_rows, tile_rows), 1)
    gradient_out[...] = total[...] + sum_terms(pieces, count, hot, hot.shape[1] - len(pieces) * count)
    copy.wait()
    mine = gradient_out[count:, :] + bundle[own:2 * own, :]
    gradient_out[count:, :] = mine

    def block(b, columns):
        values = []
        for k in range(each):
            t = pl.ds(b * each + k, 1)
            value = gradient_out[t, :] + more[pl.ds(tile_ids[k, b], 1), :]
            gradient_out[t, :] = value
            values.append(value)
        image = forward_block(tiles, values, lane, b, None)
        transpose_block(tiles, weights, image, lane, b, terms_out)
        return jnp.where(lane == b, image, columns)

    columns = lax.fori_loop(0, blocks, block, jnp.zeros((tile_rows, tile_rows), F32), unroll=16)
    image_out[...] = columns
    terms_out[count:, :] = sums_row(
        mine, bundle[2 * own + 8:3 * own + 8, :], weights[...], columns, (8, terms_out.shape[1]))


def third_kernel(shapes, late_shapes, ids, me, tiles, weights, want, bundle, total, scale, hot, gradient, departure,
                 image, *refs):
    parts, late = refs[:len(shapes)], refs[len(shapes):len(shapes) + len(late_shapes)]
    sums_out, flux_out, gradient_out, departure_out, image_out, second, tile_ids, sem = refs[len(shapes) + len(late_shapes):]
    copy = pltpu.make_async_copy(ids, tile_ids, sem)
    copy.start()
    blocks, each, tile_rows, _ = tiles.shape
    count = blocks * each
    own = want.shape[0] - count
    lane = lax.broadcasted_iota(jnp.int32, (tile_rows, tile_rows), 1)
    late, _ = layout(late_shapes, late, count + 8, own)
    pieces = layout(shapes, parts, count + 8, own)[0] + late
    sums = jnp.zeros((1, 128), F32)
    for _, ref, at in pieces:
        sums = sums + ref[at + count:at + count + 1, :128]
    step = sums[:, 0:1] / sums[:, 1:2]
    second[...] = total[...] + sum_terms(late, count, hot, hot.shape[1] - len(late) * count)
    copy.wait()
    old = gradient[count:, :]
    precision = bundle[2 * own + 8:, :]
    mine = old - step * (second[count:, :] + precision * old)
    gradient_out[...] = mine
    flux_out[...] = bundle[:own, :] - step * old
    second[:count, :] = gradient[:count, :] - step * second[:count, :]

    def block(b, columns):
        values = []
        for k in range(each):
            t = pl.ds(b * each + k, 1)
            values.append(second[t, :] - step * scale[pl.ds(tile_ids[k, b], 1), :] * gradient[t, :])
        return jnp.where(lane == b, forward_block(tiles, values, lane, b, None), columns)

    columns = lax.fori_loop(0, blocks, block, jnp.zeros((tile_rows, tile_rows), F32), unroll=16)
    row = sums_row(mine, precision, weights[...], columns, (1, 128))
    sums_out[...] = jnp.broadcast_to(row[None], sums_out.shape)
    departure_out[...] = (departure[...] - step * image[...]).T[:blocks]
    image_out[...] = columns.T[:blocks]


def last_kernel(sums, flux, gradient, departure, image, flux_out, departure_out):
    total = jnp.sum(sums[...], axis=0)
    step = total[:, 0:1] / total[:, 1:2]
    flux_out[...] = flux[...] - step * gradient[...]
    departure_out[...] = departure[...] - step * image[...]


def body(footprints, tile_index, observed, week_ids, week_weight, counts, flux_start, flux_prior, prior_precision):
    n = lax.axis_size("obs")
    blocks, each, tile_rows, cols = footprints.shape
    own = flux_start.shape[0]
    count = blocks * each
    square = (tile_rows, tile_rows)
    place = (tile_index.T, lax.axis_index("obs").astype(jnp.int32)[None])

    def in_hbm(*arrays):
        return [pltpu.with_memory_space_constraint(x, pltpu.HBM) for x in arrays]

    pitch = 3 * own + 8
    bundle, want = call(
        bundle_kernel, [HBM, SMEM] + [HBM] * 3, [(pitch, cols), (count + own, 128)],
        [pltpu.VMEM((own, cols), F32), pltpu.SMEM((each, blocks), jnp.int32), pltpu.SemaphoreType.DMA((4,))],
        flops=10000, moved=12 * own * cols,
    )(*in_hbm(place[0]), place[1], *in_hbm(flux_start, flux_prior, prior_precision))
    weights, observed_t, tiles = call(
        prepare_kernel, [SMEM] + [HBM] * 4, [square, square, footprints.shape],
        [pltpu.SMEM(week_weight.shape, F32), pltpu.VMEM(week_ids.shape, jnp.int32), pltpu.VMEM(observed.shape, F32),
         pltpu.SemaphoreType.DMA((3 + blocks // 2,))],
        flops=10000, moved=8 * footprints.size, pinned=True,
    )(counts, *in_hbm(week_weight, week_ids, observed, footprints))

    parts, rest = spread_bundle(flux_start, bundle, own, weights)
    tiles = pltpu.with_memory_space_constraint(tiles, pltpu.VMEM)

    def shapes(parts):
        return [(p.masks, p.rest_masks) for p in parts]

    def arrays(parts):
        return [p.array for p in parts]

    def split(parts):
        return [p for i, p in enumerate(parts) if i % 4 != 3], parts[3::4]

    ids_scratch = [pltpu.SMEM((each, blocks), jnp.int32), pltpu.SemaphoreType.DMA]
    hot_shape = (count + own, n * count)
    whole = (n * own, cols)
    work = dict(flops=4 * footprints.size, moved=4 * footprints.size)
    terms, departure = call(
        functools.partial(first_kernel, shapes(parts)), [VMEM, SMEM] + [VMEM] * (3 + len(parts)),
        [(count, cols), square], [pltpu.VMEM(whole, F32), *ids_scratch], **work,
    )(*place, tiles, weights, observed_t, *arrays(parts))

    parts = spread(terms, rest, 0, own + 8)
    early, late = split(parts)
    total, more, hot = call(
        functools.partial(early_kernel, shapes(early), count, own + 8, count, True), [SMEM] + [VMEM] * (1 + len(early)),
        [(count + own, cols), whole, hot_shape], moved=4 * n * count * cols,
    )(place[1], want, *arrays(early))
    terms, gradient, image = call(
        functools.partial(second_kernel, shapes(late)), [VMEM, SMEM] + [VMEM] * (7 + len(late)),
        [(count + 8, cols), (count + own, cols), square], ids_scratch, **work,
    )(*place, tiles, weights, want, bundle, total, more, hot, *arrays(late))

    parts = spread(terms, rest, own + 8, own)
    early, late = split(parts)
    total, scale = call(
        functools.partial(early_kernel, shapes(early), count + 8, own, count, False),
        [SMEM] + [VMEM] * (2 + len(early)), [(count + own, cols), whole], moved=4 * n * count * cols,
    )(place[1], want, *arrays(early), hot)
    sums, flux, gradient, departure, image = call(
        functools.partial(third_kernel, shapes(early), shapes(late)),
        [VMEM, SMEM] + [VMEM] * (10 + len(early) + len(late)),
        [(n, 1, 128), (own, cols), (own, cols), (blocks, tile_rows), (blocks, tile_rows)],
        [pltpu.VMEM((count + own, cols), F32), *ids_scratch], **work,
    )(*place, tiles, weights, want, bundle, total, scale, hot, gradient, departure, image, *arrays(early), *arrays(late))

    sums = lax.all_to_all(sums, "obs", 0, 0)
    flux, departure = call(
        last_kernel, [VMEM] * 5, [(own, cols), (blocks, tile_rows)], flops=20000, moved=200000,
    )(sums, flux, gradient, departure, image)
    return flux, departure


def solution(mesh):
    rows = P(("groups", "obs"), None)
    return jax.shard_map(
        body,
        mesh=mesh,
        in_specs=(
            P(("groups", "obs"), None, None, None), rows, rows, rows,
            P("groups"), P(("groups", "obs")), rows, rows, rows,
        ),
        out_specs=(rows, rows),
        check_vma=False,
    )
```
